256 devices in a mesh: seq: 32 (over z, x_hi, core), head: 8 (over x_lo, y).
Axes of the slice: x: 4 (x_hi: 2, x_lo: 2; x = x_hi * 2 + x_lo), y: 4, z: 8, core: 2. Of those that a mesh axis runs over, the one named last changes fastest.
Arguments:
- queries: bfloat16 [128, 2, 8192], P('seq', None, 'head'), may hold values from -7 to 7
- prefix_keys: bfloat16 [131072, 8, 128], P('seq', 'head'), may hold values from -15 to 15
- prefix_values: bfloat16 [131072, 8, 128], P('seq', 'head'), may hold values from -12 to 12
- suffix_keys: bfloat16 [128, 4096, 8, 128], P('seq', None, 'head'), may hold values from -19 to 19
- suffix_values: bfloat16 [128, 4096, 8, 128], P('seq', None, 'head'), may hold values from -12 to 12
- new_keys: bfloat16 [128, 2, 8, 128], P('seq', None, 'head'), may hold values from -8 to 8
- new_values: bfloat16 [128, 2, 8, 128], P('seq', None, 'head'), may hold values from -12 to 12
- suffix_lengths: int32 [128], P('seq'), may hold values from 1 to 4096, 262144 in all
- out_weight: bfloat16 [8192, 8192], P('head', 'seq'), may hold values from -0.0625 to 0.0625
Outputs:
- layer_output: bfloat16 [128, 2, 8192], P('head', None, 'seq')
The draws below stay inside these ranges and needn't reach their ends.
Inputs may be any that keep to these rules, and one draw needn't show every extreme that they name: `suffix_lengths`: the longest suffix holds exactly 4096 tokens.
All inputs are finite; a program needn't handle non-finite values. No bound on the sum of `suffix_lengths` on one device may be relied on, other than what follows from the above.
Results may differ from the reference program's by a relative error of at most 0.015.
Values may be sent and summed in bfloat16 or wider, within the bound.
No kernel may reach another device: no remote copies, remote signals or barrier semaphores. Data moves between devices by JAX's collectives and lax.ppermute only.
A program may use at most 192 MiB of HBM per device.

```python
import math
import jax
import jax.numpy as jnp
import numpy as np
from jax import lax

D = 8192
HEADS = 64
KV_HEADS = 8
HEAD_DIM = 128
NEW = 2
SUFFIX_MAX = 4096
PREFIX = 131072
REQUESTS = 128


def shared_base(key):
    query_key = jax.random.fold_in(key, 0)
    common = jnp.clip(jax.random.normal(query_key, (REQUESTS, NEW, HEADS * HEAD_DIM), jnp.float32), -5.0, 5.0)
    return common


def draw_queries(key, part):
    common = shared_base(key)
    return common.astype(jnp.bfloat16)


def draw_prefix_keys(key, part):
    key = jax.random.fold_in(key, 23)
    return jnp.clip(2.5 * jax.random.normal(key, (PREFIX, KV_HEADS, HEAD_DIM), jnp.float32), -15.0, 15.0).astype(jnp.bfloat16)


def draw_new_keys(key, part):
    common = shared_base(key)
    key = jax.random.fold_in(key, 37)
    aligned = common.reshape(REQUESTS, NEW, KV_HEADS, HEADS // KV_HEADS, HEAD_DIM)[:, :, :, 0, :]
    jitter = 0.5 * jax.random.normal(key, aligned.shape, jnp.float32)
    return jnp.clip(1.15 * aligned + jitter, -8.0, 8.0).astype(jnp.bfloat16)


def steps_of(key, dims, cuts, smallest, top_value):
    def one(axis_at, shards_of):
        draws = jax.random.uniform(jax.random.fold_in(jax.random.fold_in(key, 6), axis_at), (shards_of,), jnp.float32, smallest / len(cuts), top_value / len(cuts))
        return jnp.repeat(jnp.exp(draws), dims[axis_at] // shards_of).reshape((-1,) + (1,) * (len(dims) - axis_at - 1))

    loudness = one(*cuts[0])
    for cut in cuts[1:]:
        loudness = loudness * one(*cut)
    return loudness


def length_profile(number_of, total, bound, slope):
    weights = [(1 << 20) // math.isqrt(grade ** slope) + 1 for grade in range(2, number_of + 1)]
    surplus, given = total - bound - (number_of - 1), [1] * (number_of - 1)
    while surplus > 0:
        candidates = [i for i in range(number_of - 1) if given[i] < bound]
        pool, budget = sum([weights[i] for i in candidates]), surplus
        for i in candidates:
            addition = min(bound - given[i], max(1, budget * weights[i] // pool), surplus)
            given[i] = given[i] + addition
            surplus = surplus - addition
    return np.array([bound] + given)


def uneven(rng, amount, total, limit, lean):
    if amount == 2:
        one = jax.random.randint(rng, (), max(1, total - limit), min(limit, total - 1) + 1)
        return jnp.stack([one, total - one])
    sizes = jnp.asarray(length_profile(amount, total, limit, lean), jnp.int32)
    pairs = (amount - 1) // 2
    source_of, taker = sizes[1:1 + 2 * pairs:2], sizes[2:2 + 2 * pairs:2]
    margin = jnp.minimum(source_of - 1, limit - taker)
    passed = jax.random.randint(jax.random.fold_in(rng, 1), (pairs,), 0, 1 << 20) % (margin + 1)
    sizes = sizes.at[1:1 + 2 * pairs:2].set(source_of - passed).at[2:2 + 2 * pairs:2].set(taker + passed)
    return sizes[jax.random.permutation(jax.random.fold_in(rng, 2), amount)]


def scatter_about(stream_key, shape, width, reach, shards=(), held_as=jnp.bfloat16):
    entries = width * jax.random.normal(stream_key, shape, jnp.float32)
    if shards:
        entries = entries * steps_of(stream_key, shape, shards, -0.22, 0.18)
    return jnp.clip(entries, -reach, reach).astype(held_as)


def setup_inputs(seed: int = 0) -> dict:
    streams_of = jax.random.split(jax.random.key(seed), 10)
    return {
        "queries": draw_queries(jax.random.fold_in(streams_of[9], 71), 0),
        "prefix_keys": draw_prefix_keys(jax.random.fold_in(streams_of[9], 71), 0),
        "prefix_values": scatter_about(streams_of[2], (PREFIX, KV_HEADS, HEAD_DIM), 2.0, 12.0, ((0, 32), (1, 8))),
        "suffix_keys": scatter_about(streams_of[3], (REQUESTS, SUFFIX_MAX, KV_HEADS, HEAD_DIM), 3.2, 19.0, ((0, 32), (2, 8))),
        "suffix_values": scatter_about(streams_of[4], (REQUESTS, SUFFIX_MAX, KV_HEADS, HEAD_DIM), 2.0, 12.0, ((0, 32), (2, 8))),
        "new_keys": draw_new_keys(jax.random.fold_in(streams_of[9], 71), 0),
        "new_values": scatter_about(streams_of[6], (REQUESTS, NEW, KV_HEADS, HEAD_DIM), 2.0, 12.0, ((0, 32), (2, 8))),
        "suffix_lengths": uneven(streams_of[7], REQUESTS, REQUESTS * SUFFIX_MAX // 2, SUFFIX_MAX, 2).astype(jnp.int32),
        "out_weight": scatter_about(streams_of[8], (HEADS * HEAD_DIM, D), (HEADS * HEAD_DIM) ** -0.5, 0.0625, ((0, 8), (1, 32))),
    }


masked_score = -1.0e30


def rounded(weights):
    return lax.optimization_barrier(weights.astype(jnp.bfloat16)).astype(jnp.float32)


def reference(queries, prefix_keys, prefix_values, suffix_keys, suffix_values, new_keys, new_values, suffix_lengths, out_weight):
    group_size = HEADS // KV_HEADS
    score_scale = HEAD_DIM ** -0.5
    by_head = queries.reshape(REQUESTS, NEW, KV_HEADS, group_size, HEAD_DIM)
    allowed = (jnp.arange(SUFFIX_MAX, dtype=jnp.int32)[None, :] < suffix_lengths.astype(jnp.int32)[:, None])[:, None, None, :]
    causal = (jnp.arange(NEW, dtype=jnp.int32)[:, None] >= jnp.arange(NEW, dtype=jnp.int32)[None, :])[None, :, None, :]

    def one_head(head_index):
        query_rows = lax.dynamic_index_in_dim(by_head, head_index, 2, keepdims=False)
        flat_rows = query_rows.reshape(REQUESTS * NEW * group_size, HEAD_DIM)
        key_rows = lax.dynamic_index_in_dim(prefix_keys, head_index, 1, keepdims=False)
        value_rows = lax.dynamic_index_in_dim(prefix_values, head_index, 1, keepdims=False)
        prefix_scores = jnp.dot(flat_rows, key_rows.T, preferred_element_type=jnp.float32) * score_scale
        query_wide = query_rows.astype(jnp.float32)
        suffix_key_rows = lax.dynamic_index_in_dim(suffix_keys, head_index, 2, keepdims=False).astype(jnp.float32)
        suffix_value_rows = lax.dynamic_index_in_dim(suffix_values, head_index, 2, keepdims=False).astype(jnp.float32)
        new_key_rows = lax.dynamic_index_in_dim(new_keys, head_index, 2, keepdims=False).astype(jnp.float32)
        new_value_rows = lax.dynamic_index_in_dim(new_values, head_index, 2, keepdims=False).astype(jnp.float32)
        suffix_scores = jnp.einsum("rtjd,rsd->rtjs", query_wide, suffix_key_rows, precision=lax.Precision.HIGHEST) * score_scale
        new_scores = jnp.einsum("rtjd,rud->rtju", query_wide, new_key_rows, precision=lax.Precision.HIGHEST) * score_scale
        prefix_peak = jnp.max(prefix_scores, axis=1).reshape(REQUESTS, NEW, group_size)
        suffix_peak = jnp.max(jnp.where(allowed, suffix_scores, masked_score), axis=-1)
        new_peak = jnp.max(jnp.where(causal, new_scores, masked_score), axis=-1)
        peak = jnp.maximum(prefix_peak, jnp.maximum(suffix_peak, new_peak))
        prefix_weights = jnp.exp(prefix_scores - peak.reshape(REQUESTS * NEW * group_size)[:, None])
        suffix_weights = jnp.where(allowed, jnp.exp(suffix_scores - peak[..., None]), 0.0)
        new_weights = jnp.where(causal, jnp.exp(new_scores - peak[..., None]), 0.0)
        totals = jnp.sum(prefix_weights, axis=1).reshape(REQUESTS, NEW, group_size) + jnp.sum(suffix_weights, axis=-1) + jnp.sum(new_weights, axis=-1)
        numerator = jnp.dot(prefix_weights.astype(jnp.bfloat16), value_rows, preferred_element_type=jnp.float32).reshape(REQUESTS, NEW, group_size, HEAD_DIM)
        numerator = numerator + jnp.einsum("rtjs,rsd->rtjd", rounded(suffix_weights), suffix_value_rows, precision=lax.Precision.HIGHEST)
        numerator = numerator + jnp.einsum("rtju,rud->rtjd", rounded(new_weights), new_value_rows, precision=lax.Precision.HIGHEST)
        return (numerator / totals[..., None]).astype(jnp.bfloat16)

    attended = lax.map(one_head, jnp.arange(KV_HEADS, dtype=jnp.int32))
    attended = jnp.transpose(attended, (1, 2, 0, 3, 4)).reshape(REQUESTS * NEW, HEADS * HEAD_DIM)
    layer_output = jnp.dot(attended, out_weight, preferred_element_type=jnp.float32)
    return layer_output.reshape(REQUESTS, NEW, D).astype(jnp.bfloat16)
```

```python
import functools

import jax
import jax.numpy as jnp
from jax import lax
from jax.experimental import pallas as pl
from jax.experimental.pallas import tpu as pltpu
from jax.sharding import PartitionSpec as P

LOW = -1.0e30
LOG2E = 1.4426950408889634
STAT_ROWS = 16


def dot_rows(left, right):
    return lax.dot_general(
        left, right, (((1,), (1,)), ((), ())), preferred_element_type=jnp.float32
    )


def split_bf16(value):
    high = value.astype(jnp.bfloat16)
    rest = value - high.astype(jnp.float32)
    middle = rest.astype(jnp.bfloat16)
    low = (rest - middle.astype(jnp.float32)).astype(jnp.bfloat16)
    return high, middle, low


def prefix_kernel(query_ref, key_ref, value_ref, out_ref, *, key_block, group, scale):
    query_rows = query_ref[...]
    count, head_dim = query_rows.shape
    positions = key_ref.shape[0]
    top = jnp.full((count, 1), LOW, jnp.float32)
    total = jnp.zeros((count, head_dim), jnp.float32)
    acc = jnp.zeros((count, head_dim), jnp.float32)
    for start in range(0, positions, key_block):
        scores = dot_rows(query_rows, key_ref[start : start + key_block, :]) * scale
        new_top = jnp.maximum(top, jnp.max(scores, axis=1, keepdims=True))
        weights = jnp.exp2(scores - new_top)
        rescale = jnp.exp2(top - new_top)
        part = weights[:, :head_dim]
        for lane in range(head_dim, key_block, head_dim):
            part = part + weights[:, lane : lane + head_dim]
        total = total * rescale + part
        acc = acc * rescale + jnp.dot(
            weights.astype(jnp.bfloat16),
            value_ref[start : start + key_block, :],
            preferred_element_type=jnp.float32,
        )
        top = new_top
    total = jnp.sum(total, axis=1, keepdims=True)
    mean = (acc / total).astype(jnp.bfloat16)
    row = lax.broadcasted_iota(jnp.int32, (group, head_dim), 0)
    lane = lax.broadcasted_iota(jnp.int32, (group, head_dim), 1)
    for index in range(count // group):
        rows = slice(index * group, (index + 1) * group)
        stat = jnp.where(lane == row, top[rows], 0.0) + jnp.where(
            lane == row + group, total[rows], 0.0
        )
        stat = jnp.sum(stat, axis=0, keepdims=True)
        high, middle, low = split_bf16(stat)
        out_ref[index, :group, :] = mean[rows]
        tile_row = lax.broadcasted_iota(jnp.int32, (STAT_ROWS, head_dim), 0)
        tile = jnp.where(tile_row == 0, high.astype(jnp.float32), 0.0)
        tile = tile + jnp.where(tile_row == 1, middle.astype(jnp.float32), 0.0)
        tile = tile + jnp.where(tile_row == 2, low.astype(jnp.float32), 0.0)
        out_ref[index, group:, :] = tile.astype(jnp.bfloat16)


def prefix_parts(query_rows, key_rows, value_rows, group, scale):
    count, head_dim = query_rows.shape
    row_block = min(512, count)
    owners = row_block // group
    return pl.pallas_call(
        functools.partial(
            prefix_kernel, key_block=min(512, key_rows.shape[0]), group=group, scale=scale
        ),
        grid=(count // row_block,),
        in_specs=[
            pl.BlockSpec((row_block, head_dim), lambda i: (i, 0)),
            pl.BlockSpec(key_rows.shape, lambda i: (0, 0)),
            pl.BlockSpec(value_rows.shape, lambda i: (0, 0)),
        ],
        out_specs=pl.BlockSpec((owners, group + STAT_ROWS, head_dim), lambda i: (i, 0, 0)),
        out_shape=jax.ShapeDtypeStruct(
            (count // group, group + STAT_ROWS, head_dim), jnp.bfloat16
        ),
        compiler_params=pltpu.CompilerParams(vmem_limit_bytes=40 * 2**20),
        name="prefix_parts",
    )(query_rows, key_rows, value_rows)


def suffix_kernel(
    length_ref, query_ref, key_ref, value_ref, new_key_ref, new_value_ref,
    mean_ref, top_ref, total_ref, acc_ref, *, key_block, group_size, scale,
):
    request = pl.program_id(0)
    block = pl.program_id(1)
    length = length_ref[request]
    query_rows = query_ref[0]
    rows, head_dim = query_rows.shape

    @pl.when(block == 0)
    def _():
        new_keys = new_key_ref[0]
        count = new_keys.shape[0]
        scores = dot_rows(query_rows, new_keys) * scale
        step = lax.broadcasted_iota(jnp.int32, (rows, count), 0) // group_size
        slot = lax.broadcasted_iota(jnp.int32, (rows, count), 1)
        allowed = step >= slot
        scores = jnp.where(allowed, scores, LOW)
        top = jnp.max(scores, axis=1, keepdims=True)
        weights = jnp.where(allowed, jnp.exp2(scores - top), 0.0)
        rounded = weights.astype(jnp.bfloat16).astype(jnp.float32)
        values = new_value_ref[0].astype(jnp.float32)
        acc = rounded[:, 0:1] * values[0:1]
        for slot_index in range(1, count):
            acc = acc + rounded[:, slot_index : slot_index + 1] * values[slot_index : slot_index + 1]
        acc_ref[...] = acc
        top_ref[0] = jnp.broadcast_to(top, (rows, head_dim))
        total_ref[0] = jnp.broadcast_to(jnp.sum(weights, axis=1, keepdims=True), (rows, head_dim))

    @pl.when(block * key_block < length)
    def _():
        top = top_ref[0][:, 0:1]
        scores = dot_rows(query_rows, key_ref[0]) * scale
        slot = block * key_block + lax.broadcasted_iota(jnp.int32, scores.shape, 1)
        scores = jnp.where(slot < length, scores, LOW)
        new_top = jnp.maximum(top, jnp.max(scores, axis=1, keepdims=True))
        weights = jnp.exp2(scores - new_top)
        rescale = jnp.exp2(top - new_top)
        total_ref[0] = total_ref[0] * rescale + jnp.sum(weights, axis=1, keepdims=True)
        acc_ref[...] = acc_ref[...] * rescale + jnp.dot(
            weights.astype(jnp.bfloat16), value_ref[0], preferred_element_type=jnp.float32
        )
        top_ref[0] = jnp.broadcast_to(new_top, (rows, head_dim))

    @pl.when(block == pl.num_programs(1) - 1)
    def _():
        mean_ref[0] = acc_ref[...] / total_ref[0]


def suffix_part(query_rows, keys, values, new_keys, new_values, lengths, group_size, scale):
    requests, rows, head_dim = query_rows.shape
    slots = keys.shape[1]
    count = new_keys.shape[1]
    key_block = min(2048, slots)

    def held(r, b, length_ref):
        return (r, jnp.minimum(b, (length_ref[r] - 1) // key_block), 0)

    own = lambda r, b, length_ref: (r, 0, 0)
    shape = jax.ShapeDtypeStruct((requests, rows, head_dim), jnp.float32)
    return pl.pallas_call(
        functools.partial(suffix_kernel, key_block=key_block, group_size=group_size, scale=scale),
        grid_spec=pltpu.PrefetchScalarGridSpec(
            num_scalar_prefetch=1,
            grid=(requests, slots // key_block),
            in_specs=[
                pl.BlockSpec((1, rows, head_dim), own),
                pl.BlockSpec((1, key_block, head_dim), held),
                pl.BlockSpec((1, key_block, head_dim), held),
                pl.BlockSpec((1, count, head_dim), own),
                pl.BlockSpec((1, count, head_dim), own),
            ],
            out_specs=[pl.BlockSpec((1, rows, head_dim), own)] * 3,
            scratch_shapes=[pltpu.VMEM((rows, head_dim), jnp.float32)],
        ),
        out_shape=[shape] * 3,
        compiler_params=pltpu.CompilerParams(vmem_limit_bytes=24 * 2**20),
        name="suffix_part",
    )(lengths, query_rows, keys, values, new_keys, new_values)


def combine_kernel(part_ref, mean_ref, top_ref, total_ref, out_ref):
    senders, height, head_dim = part_ref.shape
    rows = height - STAT_ROWS
    stat = jnp.sum(part_ref[:, rows : rows + STAT_ROWS, :].astype(jnp.float32), axis=1)
    stat = stat.T
    own_top = top_ref[...][:, 0:1]
    own_total = total_ref[...][:, 0:1]
    tops, totals = stat[:rows], stat[rows : 2 * rows]
    peak = jnp.maximum(jnp.max(tops, axis=1, keepdims=True), own_top)
    weights = jnp.exp2(tops - peak) * totals
    own = jnp.exp2(own_top - peak) * own_total
    total = jnp.sum(weights, axis=1, keepdims=True) + own
    acc = mean_ref[...] * own
    for sender in range(senders):
        acc = acc + part_ref[sender, :rows, :].astype(jnp.float32) * weights[:, sender : sender + 1]
    out_ref[...] = (acc / total).astype(jnp.bfloat16)


def combine(parts, mean, top, total):
    rows, head_dim = mean.shape
    return pl.pallas_call(
        combine_kernel,
        out_shape=jax.ShapeDtypeStruct((rows, head_dim), jnp.bfloat16),
        name="combine_parts",
    )(parts, mean, top, total)


def shards(
    queries, prefix_keys, prefix_values, suffix_keys, suffix_values, new_keys, new_values,
    suffix_lengths, out_weight,
):
    owned, steps, row_width = queries.shape
    head_dim = prefix_keys.shape[2]
    group_size = row_width // head_dim
    group = owned * steps * group_size
    scale = head_dim**-0.5 * LOG2E
    everyone = owned * lax.axis_size("seq")
    own_rows = queries.reshape(group, head_dim)
    gathered = lax.all_gather(own_rows, "seq", axis=0, tiled=True)
    mean, top, total = suffix_part(
        own_rows.reshape(owned, steps * group_size, head_dim),
        suffix_keys[:, :, 0, :], suffix_values[:, :, 0, :],
        new_keys[:, :, 0, :], new_values[:, :, 0, :], suffix_lengths, group_size, scale,
    )
    parts = prefix_parts(gathered, prefix_keys[:, 0, :], prefix_values[:, 0, :], group, scale)
    parts = lax.all_to_all(parts, "seq", 0, 0, tiled=True)
    attended = combine(
        parts, mean.reshape(group, head_dim), top.reshape(group, head_dim),
        total.reshape(group, head_dim),
    )
    attended = attended.reshape(owned * steps, row_width)
    attended = lax.all_gather(attended, "seq", axis=0, tiled=True)
    partial = jnp.dot(attended, out_weight, preferred_element_type=jnp.float32)
    columns = out_weight.shape[1]
    heads = lax.axis_size("head")
    partial = partial.astype(jnp.bfloat16).reshape(heads, everyone * steps // heads, columns)
    partial = lax.all_to_all(partial, "head", 0, 0, tiled=True)
    summed = jnp.sum(partial.astype(jnp.float32), axis=0).astype(jnp.bfloat16)
    return summed.reshape(everyone // heads, steps, columns)


def solution(mesh):
    placed = (
        P("seq", None, "head"),
        P("seq", "head", None),
        P("seq", "head", None),
        P("seq", None, "head", None),
        P("seq", None, "head", None),
        P("seq", None, "head", None),
        P("seq", None, "head", None),
        P("seq"),
        P("head", "seq"),
    )
    return jax.shard_map(
        shards, mesh=mesh, in_specs=placed, out_specs=P("head", None, "seq"), check_vma=False
    )
```

```python
import functools

import jax
import jax.numpy as jnp
from jax import lax
from jax.experimental import pallas as pl
from jax.experimental.pallas import tpu as pltpu
from jax.sharding import PartitionSpec as P

LOW = -1.0e30
LOG2E = 1.4426950408889634
STAT_ROWS = 16
TOTAL_MAX = 2.0**100


def dot_rows(left, right):
    return lax.dot_general(
        left, right, (((1,), (1,)), ((), ())), preferred_element_type=jnp.float32
    )


def split_bf16(value):
    high = value.astype(jnp.bfloat16)
    rest = value - high.astype(jnp.float32)
    middle = rest.astype(jnp.bfloat16)
    low = (rest - middle.astype(jnp.float32)).astype(jnp.bfloat16)
    return high, middle, low


def running_softmax(query_rows, key_refs, value_refs, key_block, scale):
    count, head_dim = query_rows.shape

    def advance(key_ref, value_ref):
        def step(index, state):
            top, total, acc = state
            rows = pl.ds(pl.multiple_of(index * key_block, key_block), key_block)
            scores = dot_rows(query_rows, key_ref[rows, :]) * scale
            new_top = jnp.maximum(top, jnp.max(scores, axis=1, keepdims=True))
            weights = jnp.exp2(scores - new_top)
            rescale = jnp.exp2(top - new_top)
            total = total * rescale + jnp.sum(weights, axis=1, keepdims=True)
            acc = acc * rescale + jnp.dot(
                weights.astype(jnp.bfloat16), value_ref[rows, :], preferred_element_type=jnp.float32
            )
            return new_top, total, acc

        return step

    state = (
        jnp.full((count, 1), LOW, jnp.float32),
        jnp.zeros((count, 1), jnp.float32),
        jnp.zeros((count, head_dim), jnp.float32),
    )
    for key_ref, value_ref in zip(key_refs, value_refs):
        state = lax.fori_loop(
            0, key_ref.shape[0] // key_block, advance(key_ref, value_ref), state
        )
    return state


def shifted_softmax(query_rows, key_refs, value_refs, key_block, scale):
    head_dim = query_rows.shape[1]
    ones = jnp.ones((key_block, head_dim), jnp.bfloat16)
    top = acc = None
    for key_ref, value_ref in zip(key_refs, value_refs):
        for start in range(0, key_ref.shape[0], key_block):
            scores = dot_rows(query_rows, key_ref[start : start + key_block, :]) * scale
            if top is None:
                top = jnp.max(scores, axis=1, keepdims=True)
            weights = jnp.exp2(scores - top).astype(jnp.bfloat16)
            values = jnp.concatenate([value_ref[start : start + key_block, :], ones], axis=1)
            part = jnp.dot(weights, values, preferred_element_type=jnp.float32)
            acc = part if acc is None else acc + part
    return top, acc[:, head_dim:], acc[:, :head_dim]


def prefix_kernel(
    query_ref, key_ref, value_ref, other_key_ref, other_value_ref, out_ref, top_ref, total_ref, acc_ref,
    *, key_block, group, scale,
):
    query_rows = query_ref[...]
    count, head_dim = query_rows.shape
    key_refs, value_refs = (key_ref, other_key_ref), (value_ref, other_value_ref)
    top, total, acc = shifted_softmax(query_rows, key_refs, value_refs, key_block, scale)
    top_ref[...] = jnp.broadcast_to(top, (count, head_dim))
    total_ref[...] = total
    acc_ref[...] = acc

    @pl.when(jnp.logical_not(jnp.max(total) < TOTAL_MAX))
    def _():
        top, total, acc = running_softmax(query_rows, key_refs, value_refs, key_block, scale)
        top_ref[...] = jnp.broadcast_to(top, (count, head_dim))
        total_ref[...] = jnp.broadcast_to(total, (count, head_dim))
        acc_ref[...] = acc

    row = lax.broadcasted_iota(jnp.int32, (group, head_dim), 0)
    lane = lax.broadcasted_iota(jnp.int32, (group, head_dim), 1)
    tile_row = lax.broadcasted_iota(jnp.int32, (STAT_ROWS, head_dim), 0)
    for index in range(count // group):
        rows = slice(index * group, (index + 1) * group)
        total = total_ref[rows, :]
        stat = jnp.where(lane == row, top_ref[rows, :], 0.0)
        stat = jnp.where(lane == row + group, total, stat)
        high, middle, low = split_bf16(jnp.sum(stat, axis=0, keepdims=True))
        out_ref[index, :group, :] = (acc_ref[rows, :] / total).astype(jnp.bfloat16)
        tile = jnp.where(tile_row == 0, high.astype(jnp.float32), 0.0)
        tile = jnp.where(tile_row == 1, middle.astype(jnp.float32), tile)
        tile = jnp.where(tile_row == 2, low.astype(jnp.float32), tile)
        out_ref[index, group:, :] = tile.astype(jnp.bfloat16)


def prefix_parts(query_rows, keys, values, other_keys, other_values, group, scale, row_block=1024, key_block=256):
    count, head_dim = query_rows.shape
    row_block = min(row_block, count)
    owners = row_block // group
    whole = pl.BlockSpec(keys.shape, lambda i: (0, 0))
    return pl.pallas_call(
        functools.partial(
            prefix_kernel, key_block=min(key_block, keys.shape[0]), group=group, scale=scale
        ),
        grid=(count // row_block,),
        in_specs=[pl.BlockSpec((row_block, head_dim), lambda i: (i, 0))] + [whole] * 4,
        out_specs=pl.BlockSpec((owners, group + STAT_ROWS, head_dim), lambda i: (i, 0, 0)),
        out_shape=jax.ShapeDtypeStruct(
            (count // group, group + STAT_ROWS, head_dim), jnp.bfloat16
        ),
        scratch_shapes=[pltpu.VMEM((row_block, head_dim), jnp.float32)] * 3,
        compiler_params=pltpu.CompilerParams(vmem_limit_bytes=40 * 2**20),
        name="prefix_parts",
    )(query_rows, keys, values, other_keys, other_values)


def suffix_kernel(
    length_ref, query_ref, key_ref, value_ref, new_key_ref, new_value_ref,
    mean_ref, top_ref, total_ref, acc_ref, *, key_block, group_size, scale,
):
    request = pl.program_id(0)
    block = pl.program_id(1)
    length = length_ref[request]
    query_rows = query_ref[0]
    rows, head_dim = query_rows.shape

    @pl.when(block == 0)
    def _():
        new_keys = new_key_ref[0]
        count = new_keys.shape[0]
        scores = dot_rows(query_rows, new_keys) * scale
        step = lax.broadcasted_iota(jnp.int32, (rows, count), 0) // group_size
        slot = lax.broadcasted_iota(jnp.int32, (rows, count), 1)
        allowed = step >= slot
        scores = jnp.where(allowed, scores, LOW)
        top = jnp.max(scores, axis=1, keepdims=True)
        weights = jnp.where(allowed, jnp.exp2(scores - top), 0.0)
        rounded = weights.astype(jnp.bfloat16).astype(jnp.float32)
        values = new_value_ref[0].astype(jnp.float32)
        acc = rounded[:, 0:1] * values[0:1]
        for slot_index in range(1, count):
            acc = acc + rounded[:, slot_index : slot_index + 1] * values[slot_index : slot_index + 1]
        acc_ref[...] = acc
        top_ref[0] = jnp.broadcast_to(top, (rows, head_dim))
        total_ref[0] = jnp.broadcast_to(jnp.sum(weights, axis=1, keepdims=True), (rows, head_dim))

    @pl.when(block * key_block < length)
    def _():
        top = top_ref[0][:, 0:1]
        scores = dot_rows(query_rows, key_ref[0]) * scale
        slot = block * key_block + lax.broadcasted_iota(jnp.int32, scores.shape, 1)
        scores = jnp.where(slot < length, scores, LOW)
        new_top = jnp.maximum(top, jnp.max(scores, axis=1, keepdims=True))
        weights = jnp.exp2(scores - new_top)
        rescale = jnp.exp2(top - new_top)
        total_ref[0] = total_ref[0] * rescale + jnp.sum(weights, axis=1, keepdims=True)
        acc_ref[...] = acc_ref[...] * rescale + jnp.dot(
            weights.astype(jnp.bfloat16), value_ref[0], preferred_element_type=jnp.float32
        )
        top_ref[0] = jnp.broadcast_to(new_top, (rows, head_dim))

    @pl.when(block == pl.num_programs(1) - 1)
    def _():
        mean_ref[0] = acc_ref[...] / total_ref[0]


def suffix_part(query_rows, keys, values, new_keys, new_values, lengths, group_size, scale):
    requests, rows, head_dim = query_rows.shape
    slots = keys.shape[1]
    count = new_keys.shape[1]
    key_block = min(2048, slots)

    def held(r, b, length_ref):
        return (r, jnp.minimum(b, (length_ref[r] - 1) // key_block), 0)

    own = lambda r, b, length_ref: (r, 0, 0)
    shape = jax.ShapeDtypeStruct((requests, rows, head_dim), jnp.float32)
    return pl.pallas_call(
        functools.partial(suffix_kernel, key_block=key_block, group_size=group_size, scale=scale),
        grid_spec=pltpu.PrefetchScalarGridSpec(
            num_scalar_prefetch=1,
            grid=(requests, slots // key_block),
            in_specs=[
                pl.BlockSpec((1, rows, head_dim), own),
                pl.BlockSpec((1, key_block, head_dim), held),
                pl.BlockSpec((1, key_block, head_dim), held),
                pl.BlockSpec((1, count, head_dim), own),
                pl.BlockSpec((1, count, head_dim), own),
            ],
            out_specs=[pl.BlockSpec((1, rows, head_dim), own)] * 3,
            scratch_shapes=[pltpu.VMEM((rows, head_dim), jnp.float32)],
        ),
        out_shape=[shape] * 3,
        compiler_params=pltpu.CompilerParams(vmem_limit_bytes=24 * 2**20),
        name="suffix_part",
    )(lengths, query_rows, keys, values, new_keys, new_values)


def combine_kernel(part_ref, mean_ref, top_ref, total_ref, out_ref):
    senders, height, head_dim = part_ref.shape
    rows = height - STAT_ROWS
    stat = jnp.sum(part_ref[:, rows : rows + STAT_ROWS, :].astype(jnp.float32), axis=1)
    stat = stat.T
    own_top = top_ref[...][:, 0:1]
    own_total = total_ref[...][:, 0:1]
    tops, totals = stat[:rows], stat[rows : 2 * rows]
    peak = jnp.maximum(jnp.max(tops, axis=1, keepdims=True), own_top)
    weights = jnp.exp2(tops - peak) * totals
    own = jnp.exp2(own_top - peak) * own_total
    total = jnp.sum(weights, axis=1, keepdims=True) + own
    acc = mean_ref[...] * own
    for sender in range(senders):
        acc = acc + part_ref[sender, :rows, :].astype(jnp.float32) * weights[:, sender : sender + 1]
    out_ref[...] = (acc / total).astype(jnp.bfloat16)


def combine(parts, mean, top, total):
    rows, head_dim = mean.shape
    return pl.pallas_call(
        combine_kernel,
        out_shape=jax.ShapeDtypeStruct((rows, head_dim), jnp.bfloat16),
        name="combine_parts",
    )(parts, mean, top, total)


def shards(
    queries, prefix_keys, prefix_values, suffix_keys, suffix_values, new_keys, new_values,
    suffix_lengths, out_weight,
):
    owned, steps, row_width = queries.shape
    head_dim = prefix_keys.shape[2]
    group_size = row_width // head_dim
    group = owned * steps * group_size
    scale = head_dim**-0.5 * LOG2E
    everyone = owned * lax.axis_size("seq")
    devices = lax.axis_size("seq")
    sharers = devices // 2
    same_core = [list(range(core, devices, 2)) for core in range(2)]
    swap_cores = [(index, index ^ 1) for index in range(devices)]
    own_rows = queries.reshape(group, head_dim)
    keys, values = prefix_keys[:, 0, :], prefix_values[:, 0, :]
    gathered = lax.all_to_all(
        jnp.tile(own_rows, (sharers, 1)), "seq", 0, 0, axis_index_groups=same_core, tiled=True
    )
    other_keys = lax.ppermute(keys, "seq", swap_cores)
    other_values = lax.ppermute(values, "seq", swap_cores)
    mean, top, total = suffix_part(
        own_rows.reshape(owned, steps * group_size, head_dim),
        suffix_keys[:, :, 0, :], suffix_values[:, :, 0, :],
        new_keys[:, :, 0, :], new_values[:, :, 0, :], suffix_lengths, group_size, scale,
    )
    parts = prefix_parts(gathered, keys, values, other_keys, other_values, group, scale)
    parts = lax.all_to_all(parts, "seq", 0, 0, axis_index_groups=same_core, tiled=True)
    attended = combine(
        parts, mean.reshape(group, head_dim), top.reshape(group, head_dim),
        total.reshape(group, head_dim),
    )
    attended = attended.reshape(owned * steps, row_width)
    attended = lax.all_to_all(
        jnp.tile(attended, (sharers, 1)), "seq", 0, 0, axis_index_groups=same_core, tiled=True
    )
    other_attended = lax.ppermute(attended, "seq", swap_cores)
    core = lax.axis_index("seq") % 2
    even = jnp.where(core == 0, attended, other_attended)
    odd = jnp.where(core == 0, other_attended, attended)
    attended = jnp.stack(
        [rows.reshape(sharers, owned * steps, row_width) for rows in (even, odd)], axis=1
    ).reshape(everyone * steps, row_width)
    partial = jnp.dot(attended, out_weight, preferred_element_type=jnp.float32)
    columns = out_weight.shape[1]
    heads = lax.axis_size("head")
    partial = partial.astype(jnp.bfloat16).reshape(heads, everyone * steps // heads, columns)
    partial = lax.all_to_all(partial, "head", 0, 0, tiled=True)
    summed = jnp.sum(partial.astype(jnp.float32), axis=0).astype(jnp.bfloat16)
    return summed.reshape(everyone // heads, steps, columns)


def solution(mesh):
    placed = (
        P("seq", None, "head"),
        P("seq", "head", None),
        P("seq", "head", None),
        P("seq", None, "head", None),
        P("seq", None, "head", None),
        P("seq", None, "head", None),
        P("seq", None, "head", None),
        P("seq"),
        P("head", "seq"),
    )
    return jax.shard_map(
        shards, mesh=mesh, in_specs=placed, out_specs=P("head", None, "seq"), check_vma=False
    )
```

```python
import functools

import jax
import jax.numpy as jnp
from jax import lax
from jax.experimental import pallas as pl
from jax.experimental.pallas import tpu as pltpu
from jax.sharding import PartitionSpec as P

LOW = -1.0e30
LOG2E = 1.4426950408889634
STAT_ROWS = 16
TOTAL_MAX = 2.0**100


def dot_rows(left, right):
    return lax.dot_general(
        left, right, (((1,), (1,)), ((), ())), preferred_element_type=jnp.float32
    )


def split_bf16(value):
    high = value.astype(jnp.bfloat16)
    rest = value - high.astype(jnp.float32)
    middle = rest.astype(jnp.bfloat16)
    low = (rest - middle.astype(jnp.float32)).astype(jnp.bfloat16)
    return high, middle, low


def running_softmax(query_rows, key_refs, value_refs, key_block, scale):
    count, head_dim = query_rows.shape

    def advance(key_ref, value_ref):
        def step(index, state):
            top, total, acc = state
            rows = pl.ds(pl.multiple_of(index * key_block, key_block), key_block)
            scores = dot_rows(query_rows, key_ref[rows, :]) * scale
            new_top = jnp.maximum(top, jnp.max(scores, axis=1, keepdims=True))
            weights = jnp.exp2(scores - new_top)
            rescale = jnp.exp2(top - new_top)
            total = total * rescale + jnp.sum(weights, axis=1, keepdims=True)
            acc = acc * rescale + jnp.dot(
                weights.astype(jnp.bfloat16), value_ref[rows, :], preferred_element_type=jnp.float32
            )
            return new_top, total, acc

        return step

    state = (
        jnp.full((count, 1), LOW, jnp.float32),
        jnp.zeros((count, 1), jnp.float32),
        jnp.zeros((count, head_dim), jnp.float32),
    )
    for key_ref, value_ref in zip(key_refs, value_refs):
        state = lax.fori_loop(
            0, key_ref.shape[0] // key_block, advance(key_ref, value_ref), state
        )
    return state


def shifted_softmax(query_rows, key_ref, value_ref, key_block, scale, top, acc):
    ones = jnp.ones((key_block, query_rows.shape[1]), jnp.bfloat16)
    spans = [slice(start, start + key_block) for start in range(0, key_ref.shape[0], key_block)]

    def score(span):
        return dot_rows(query_rows, key_ref[span, :]) * scale

    scores = score(spans[0])
    for index, span in enumerate(spans):
        later = score(spans[index + 1]) if index + 1 < len(spans) else None
        if top is None:
            top = jnp.max(scores, axis=1, keepdims=True)
        weights = jnp.exp2(scores - top).astype(jnp.bfloat16)
        values = jnp.concatenate([value_ref[span, :], ones], axis=1)
        part = jnp.dot(weights, values, preferred_element_type=jnp.float32)
        acc = part if acc is None else acc + part
        scores = later
    return top, acc


def first_kernel(query_ref, key_ref, value_ref, top_ref, state_ref, *, key_block, scale):
    top, acc = shifted_softmax(query_ref[...], key_ref, value_ref, key_block, scale, None, None)
    top_ref[...] = jnp.broadcast_to(top, top_ref.shape)
    state_ref[...] = acc


def second_kernel(
    query_ref, key_ref, value_ref, other_key_ref, other_value_ref, first_top_ref, state_ref, out_ref,
    top_ref, total_ref, acc_ref, *, key_block, group, scale,
):
    query_rows = query_ref[...]
    count, head_dim = query_rows.shape
    top = first_top_ref[...]
    wide = jnp.concatenate([top] * (key_block // head_dim), axis=1)
    _, acc = shifted_softmax(
        query_rows, key_ref, value_ref, key_block, scale, wide, state_ref[...]
    )
    total = acc[:, head_dim:]
    top_ref[...] = top
    total_ref[...] = total
    acc_ref[...] = acc[:, :head_dim]

    @pl.when(jnp.logical_not(jnp.max(total) < TOTAL_MAX))
    def _():
        top, total, acc = running_softmax(
            query_rows, (other_key_ref, key_ref), (other_value_ref, value_ref), key_block, scale
        )
        top_ref[...] = jnp.broadcast_to(top, (count, head_dim))
        total_ref[...] = jnp.broadcast_to(total, (count, head_dim))
        acc_ref[...] = acc

    row = lax.broadcasted_iota(jnp.int32, (group, head_dim), 0)
    lane = lax.broadcasted_iota(jnp.int32, (group, head_dim), 1)
    tile_row = lax.broadcasted_iota(jnp.int32, (STAT_ROWS, head_dim), 0)
    for index in range(count // group):
        rows = slice(index * group, (index + 1) * group)
        total = total_ref[rows, :]
        stat = jnp.where(lane == row, top_ref[rows, :], 0.0)
        stat = jnp.where(lane == row + group, total, stat)
        high, middle, low = split_bf16(jnp.sum(stat, axis=0, keepdims=True))
        out_ref[index, :group, :] = (acc_ref[rows, :] / total).astype(jnp.bfloat16)
        tile = jnp.where(tile_row == 0, high.astype(jnp.float32), 0.0)
        tile = jnp.where(tile_row == 1, middle.astype(jnp.float32), tile)
        tile = jnp.where(tile_row == 2, low.astype(jnp.float32), tile)
        out_ref[index, group:, :] = tile.astype(jnp.bfloat16)


def prefix_parts(query_rows, keys, values, other_keys, other_values, group, scale):
    count, head_dim = query_rows.shape
    positions = keys.shape[0]
    held = pl.BlockSpec(memory_space=pltpu.VMEM)
    limit = pltpu.CompilerParams(vmem_limit_bytes=32 * 2**20)
    key_block = min(256, positions)
    cost = pl.CostEstimate(
        flops=6 * count * positions * head_dim,
        bytes_accessed=4 * positions * head_dim,
        transcendentals=count * positions,
    )
    top, state = pl.pallas_call(
        functools.partial(first_kernel, key_block=key_block, scale=scale),
        in_specs=[held] * 3,
        out_specs=[held] * 2,
        out_shape=[
            jax.ShapeDtypeStruct((count, head_dim), jnp.float32),
            jax.ShapeDtypeStruct((count, 2 * head_dim), jnp.float32),
        ],
        compiler_params=limit,
        cost_estimate=cost,
        name="prefix_first",
    )(query_rows, other_keys, other_values)
    return pl.pallas_call(
        functools.partial(second_kernel, key_block=key_block, group=group, scale=scale),
        in_specs=[held] * 7,
        out_specs=held,
        out_shape=jax.ShapeDtypeStruct(
            (count // group, group + STAT_ROWS, head_dim), jnp.bfloat16
        ),
        scratch_shapes=[pltpu.VMEM((count, head_dim), jnp.float32)] * 3,
        compiler_params=limit,
        cost_estimate=cost,
        name="prefix_second",
    )(query_rows, keys, values, other_keys, other_values, top, state)


def suffix_kernel(
    length_ref, query_ref, new_key_ref, new_value_ref, key_ref, value_ref,
    mean_ref, top_ref, total_ref, key_held, value_held, sems, *, key_block, group_size, scale,
):
    requests, rows, head_dim = query_ref.shape
    blocks = key_ref.shape[1] // key_block
    pair = 2 if requests % 2 == 0 else 1

    def copies(request, block):
        span = pl.ds(block * key_block, key_block)
        return [
            pltpu.make_async_copy(
                source.at[request, span, :], target.at[request, span, :], sems.at[kind, request, block]
            )
            for kind, (source, target) in enumerate(((key_ref, key_held), (value_ref, value_held)))
        ]

    def filled(start, block):
        longest = length_ref[start]
        for request in range(start + 1, start + pair):
            longest = jnp.maximum(longest, length_ref[request])
        return block * key_block < longest

    def absorb(request, block, top, total, acc):
        span = pl.ds(block * key_block, key_block)
        scores = dot_rows(query_ref[request], key_held[request, span, :]) * scale
        slot = block * key_block + lax.broadcasted_iota(jnp.int32, scores.shape, 1)
        scores = jnp.where(slot < length_ref[request], scores, LOW)
        new_top = jnp.maximum(top, jnp.max(scores, axis=1, keepdims=True))
        weights = jnp.exp2(scores - new_top)
        rescale = jnp.exp2(top - new_top)
        total = total * rescale + jnp.sum(weights, axis=1, keepdims=True)
        acc = acc * rescale + jnp.dot(
            weights.astype(jnp.bfloat16),
            value_held[request, span, :],
            preferred_element_type=jnp.float32,
        )
        return new_top, total, acc

    def keep(request, top, total, acc):
        mean_ref[request] = acc
        top_ref[request] = jnp.broadcast_to(top, (rows, head_dim))
        total_ref[request] = jnp.broadcast_to(total, (rows, head_dim))

    for request in range(requests):
        for copy in copies(request, 0):
            copy.start()
    for block in range(1, blocks):
        for start in range(0, requests, pair):

            @pl.when(filled(start, block))
            def _(start=start, block=block):
                for request in range(start, start + pair):
                    for copy in copies(request, block):
                        copy.start()

    for request in range(requests):
        for copy in copies(request, 0):
            copy.wait()
    states = []
    for request in range(requests):
        count = new_key_ref.shape[1]
        scores = dot_rows(query_ref[request], new_key_ref[request]) * scale
        step = lax.broadcasted_iota(jnp.int32, (rows, count), 0) // group_size
        slot = lax.broadcasted_iota(jnp.int32, (rows, count), 1)
        allowed = step >= slot
        top = jnp.max(jnp.where(allowed, scores, LOW), axis=1, keepdims=True)
        weights = jnp.where(allowed, jnp.exp2(scores - top), 0.0)
        rounded = weights.astype(jnp.bfloat16).astype(jnp.float32)
        values = new_value_ref[request].astype(jnp.float32)
        acc = rounded[:, 0:1] * values[0:1]
        for index in range(1, count):
            acc = acc + rounded[:, index : index + 1] * values[index : index + 1]
        total = jnp.sum(weights, axis=1, keepdims=True)
        states.append(absorb(request, 0, top, total, acc))
    for request in range(requests):
        keep(request, *states[request])

    for block in range(1, blocks):
        for start in range(0, requests, pair):

            @pl.when(filled(start, block))
            def _(start=start, block=block):
                members = range(start, start + pair)
                for request in members:
                    for copy in copies(request, block):
                        copy.wait()
                states = [
                    absorb(
                        request, block, top_ref[request][:, 0:1], total_ref[request][:, 0:1],
                        mean_ref[request],
                    )
                    for request in members
                ]
                for request, state in zip(members, states):
                    keep(request, *state)

    mean_ref[...] = mean_ref[...] / total_ref[...]


def suffix_part(query_rows, keys, values, new_keys, new_values, lengths, group_size, scale):
    requests, rows, head_dim = query_rows.shape
    slots = keys.shape[1]
    key_block = min(2048, slots)
    held = pl.BlockSpec(memory_space=pltpu.VMEM)
    away = pl.BlockSpec(memory_space=pltpu.HBM)
    return pl.pallas_call(
        functools.partial(suffix_kernel, key_block=key_block, group_size=group_size, scale=scale),
        in_specs=[pl.BlockSpec(memory_space=pltpu.SMEM), held, held, held, away, away],
        out_specs=[held] * 3,
        out_shape=[jax.ShapeDtypeStruct((requests, rows, head_dim), jnp.float32)] * 3,
        scratch_shapes=[pltpu.VMEM(keys.shape, keys.dtype)] * 2
        + [pltpu.SemaphoreType.DMA((2, requests, slots // key_block))],
        compiler_params=pltpu.CompilerParams(vmem_limit_bytes=52 * 2**20),
        cost_estimate=pl.CostEstimate(
            flops=4 * requests * rows * slots * head_dim,
            bytes_accessed=4 * requests * slots * head_dim,
            transcendentals=requests * rows * slots,
        ),
        name="suffix_part",
    )(lengths, query_rows, new_keys, new_values, keys, values)


def combine_kernel(part_ref, mean_ref, top_ref, total_ref, out_ref, acc_ref):
    senders, height, head_dim = part_ref.shape
    rows = height - STAT_ROWS
    lines = out_ref.shape[0]
    heads = rows // lines
    stat = jnp.sum(part_ref[:, rows : rows + STAT_ROWS, :].astype(jnp.float32), axis=1)
    stat = stat.T
    own_top = top_ref[...][:, 0:1]
    own_total = total_ref[...][:, 0:1]
    tops, totals = stat[:rows], stat[rows : 2 * rows]
    peak = jnp.maximum(jnp.max(tops, axis=1, keepdims=True), own_top)
    weights = jnp.exp2(tops - peak) * totals
    own = jnp.exp2(own_top - peak) * own_total
    total = jnp.sum(weights, axis=1, keepdims=True) + own
    acc = mean_ref[...] * own
    for sender in range(senders):
        acc = acc + part_ref[sender, :rows, :].astype(jnp.float32) * weights[:, sender : sender + 1]
    acc_ref[...] = acc / total
    for head in range(heads):
        out_ref[:, head * head_dim : (head + 1) * head_dim] = acc_ref[
            pl.ds(head, lines, stride=heads), :
        ].astype(jnp.bfloat16)


def combine(parts, mean, top, total, lines):
    rows, head_dim = mean.shape
    held = pl.BlockSpec(memory_space=pltpu.VMEM)
    return pl.pallas_call(
        combine_kernel,
        in_specs=[held] * 4,
        out_specs=held,
        out_shape=jax.ShapeDtypeStruct((lines, rows // lines * head_dim), jnp.bfloat16),
        scratch_shapes=[pltpu.VMEM((rows, head_dim), jnp.float32)],
        compiler_params=pltpu.CompilerParams(vmem_limit_bytes=16 * 2**20),
        name="combine_parts",
    )(parts, mean, top, total)


def shards(
    queries, prefix_keys, prefix_values, suffix_keys, suffix_values, new_keys, new_values,
    suffix_lengths, out_weight,
):
    owned, steps, row_width = queries.shape
    head_dim = prefix_keys.shape[2]
    group_size = row_width // head_dim
    group = owned * steps * group_size
    scale = head_dim**-0.5 * LOG2E
    everyone = owned * lax.axis_size("seq")
    devices = lax.axis_size("seq")
    sharers = devices // 2
    same_core = [list(range(core, devices, 2)) for core in range(2)]
    swap_cores = [(index, index ^ 1) for index in range(devices)]
    own_rows = lax.optimization_barrier(queries.reshape(group, head_dim))
    keys, values = prefix_keys[:, 0, :], prefix_values[:, 0, :]
    gathered = lax.all_to_all(
        jnp.tile(own_rows, (sharers, 1)), "seq", 0, 0, axis_index_groups=same_core, tiled=True
    )
    other_keys = lax.ppermute(keys, "seq", swap_cores)
    other_values = lax.ppermute(values, "seq", swap_cores)
    mean, top, total = suffix_part(
        own_rows.reshape(owned, steps * group_size, head_dim),
        suffix_keys[:, :, 0, :], suffix_values[:, :, 0, :],
        new_keys[:, :, 0, :], new_values[:, :, 0, :], suffix_lengths, group_size, scale,
    )
    parts = prefix_parts(gathered, keys, values, other_keys, other_values, group, scale)
    parts = lax.all_to_all(parts, "seq", 0, 0, axis_index_groups=same_core, tiled=True)
    attended = combine(
        parts, mean.reshape(group, head_dim), top.reshape(group, head_dim),
        total.reshape(group, head_dim), owned * steps,
    )
    attended = lax.all_to_all(
        jnp.tile(attended, (sharers, 1)), "seq", 0, 0, axis_index_groups=same_core, tiled=True
    )
    other_attended = lax.ppermute(attended, "seq", swap_cores)
    core = lax.axis_index("seq") % 2
    even = jnp.where(core == 0, attended, other_attended)
    odd = jnp.where(core == 0, other_attended, attended)
    attended = jnp.stack(
        [rows.reshape(sharers, owned * steps, row_width) for rows in (even, odd)], axis=1
    ).reshape(everyone * steps, row_width)
    partial = jnp.dot(attended, out_weight, preferred_element_type=jnp.float32)
    columns = out_weight.shape[1]
    heads = lax.axis_size("head")
    partial = partial.astype(jnp.bfloat16).reshape(heads, everyone * steps // heads, columns)
    partial = lax.all_to_all(partial, "head", 0, 0, tiled=True)
    summed = jnp.sum(partial.astype(jnp.float32), axis=0).astype(jnp.bfloat16)
    return summed.reshape(everyone // heads, steps, columns)


def solution(mesh):
    placed = (
        P("seq", None, "head"),
        P("seq", "head", None),
        P("seq", "head", None),
        P("seq", None, "head", None),
        P("seq", None, "head", None),
        P("seq", None, "head", None),
        P("seq", None, "head", None),
        P("seq"),
        P("head", "seq"),
    )
    return jax.shard_map(
        shards, mesh=mesh, in_specs=placed, out_specs=P("head", None, "seq"), check_vma=False
    )
```

```python
import functools

import jax
import jax.numpy as jnp
from jax import lax
from jax.experimental import pallas as pl
from jax.experimental.pallas import tpu as pltpu
from jax.sharding import PartitionSpec as P

LOW = -1.0e30
LOG2E = 1.4426950408889634
STAT_ROWS = 16
TOTAL_MAX = 2.0**100


def dot_rows(left, right):
    return lax.dot_general(
        left, right, (((1,), (1,)), ((), ())), preferred_element_type=jnp.float32
    )


def split_bf16(value):
    high = value.astype(jnp.bfloat16)
    rest = value - high.astype(jnp.float32)
    middle = rest.astype(jnp.bfloat16)
    low = (rest - middle.astype(jnp.float32)).astype(jnp.bfloat16)
    return high, middle, low


def running_softmax(query_rows, key_refs, value_refs, key_block, scale):
    count, head_dim = query_rows.shape

    def advance(key_ref, value_ref):
        def step(index, state):
            top, total, acc = state
            rows = pl.ds(pl.multiple_of(index * key_block, key_block), key_block)
            scores = dot_rows(query_rows, key_ref[rows, :]) * scale
            new_top = jnp.maximum(top, jnp.max(scores, axis=1, keepdims=True))
            weights = jnp.exp2(scores - new_top)
            rescale = jnp.exp2(top - new_top)
            total = total * rescale + jnp.sum(weights, axis=1, keepdims=True)
            acc = acc * rescale + jnp.dot(
                weights.astype(jnp.bfloat16), value_ref[rows, :], preferred_element_type=jnp.float32
            )
            return new_top, total, acc

        return step

    state = (
        jnp.full((count, 1), LOW, jnp.float32),
        jnp.zeros((count, 1), jnp.float32),
        jnp.zeros((count, head_dim), jnp.float32),
    )
    for key_ref, value_ref in zip(key_refs, value_refs):
        state = lax.fori_loop(
            0, key_ref.shape[0] // key_block, advance(key_ref, value_ref), state
        )
    return state


def shifted_softmax(query_rows, key_ref, value_ref, key_block, scale, top, acc):
    ones = jnp.ones((key_block, query_rows.shape[1]), jnp.bfloat16)
    spans = [slice(start, start + key_block) for start in range(0, key_ref.shape[0], key_block)]

    def score(span):
        return dot_rows(query_rows, key_ref[span, :]) * scale

    scores = score(spans[0])
    for index, span in enumerate(spans):
        later = score(spans[index + 1]) if index + 1 < len(spans) else None
        if top is None:
            top = jnp.max(scores, axis=1, keepdims=True)
        weights = jnp.exp2(scores - top).astype(jnp.bfloat16)
        values = jnp.concatenate([value_ref[span, :], ones], axis=1)
        part = jnp.dot(weights, values, preferred_element_type=jnp.float32)
        acc = part if acc is None else acc + part
        scores = later
    return top, acc


def first_kernel(query_ref, key_ref, value_ref, top_ref, state_ref, *, chunk, key_block, scale):
    for start in range(0, query_ref.shape[0], chunk):
        rows = slice(start, start + chunk)
        top, acc = shifted_softmax(
            query_ref[rows, :], key_ref, value_ref, key_block, scale, None, None
        )
        top_ref[rows, :] = jnp.broadcast_to(top, (chunk, top_ref.shape[1]))
        state_ref[rows, :] = acc


def write_parts(out_ref, first, group, top, total, acc):
    head_dim = acc.shape[1]
    row = lax.broadcasted_iota(jnp.int32, (group, head_dim), 0)
    lane = lax.broadcasted_iota(jnp.int32, (group, head_dim), 1)
    tile_row = lax.broadcasted_iota(jnp.int32, (STAT_ROWS, head_dim), 0)
    for index in range(acc.shape[0] // group):
        rows = slice(index * group, (index + 1) * group)
        stat = jnp.where(lane == row, top[rows], 0.0)
        stat = jnp.where(lane == row + group, total[rows], stat)
        high, middle, low = split_bf16(jnp.sum(stat, axis=0, keepdims=True))
        out_ref[first + index, :group, :] = (acc[rows] / total[rows]).astype(jnp.bfloat16)
        tile = jnp.where(tile_row == 0, high.astype(jnp.float32), 0.0)
        tile = jnp.where(tile_row == 1, middle.astype(jnp.float32), tile)
        tile = jnp.where(tile_row == 2, low.astype(jnp.float32), tile)
        out_ref[first + index, group:, :] = tile.astype(jnp.bfloat16)


def second_kernel(
    query_ref, key_ref, value_ref, other_key_ref, other_value_ref, top_ref, state_ref, out_ref,
    part_ref, sems, *, chunk, key_block, group, scale,
):
    count, head_dim = query_ref.shape
    owners = chunk // group
    copies = []
    largest = None
    for start in range(0, count, chunk):
        rows = slice(start, start + chunk)
        top = top_ref[rows, :]
        wide = jnp.concatenate([top] * (key_block // head_dim), axis=1)
        _, acc = shifted_softmax(
            query_ref[rows, :], key_ref, value_ref, key_block, scale, wide, state_ref[rows, :]
        )
        total = acc[:, head_dim:]
        largest = total if largest is None else jnp.maximum(largest, total)
        write_parts(part_ref, start // group, group, top, total, acc[:, :head_dim])
        span = pl.ds(start // group, owners)
        copy = pltpu.make_async_copy(part_ref.at[span], out_ref.at[span], sems.at[start // chunk])
        copy.start()
        copies.append(copy)
    for copy in copies:
        copy.wait()

    @pl.when(jnp.logical_not(jnp.max(largest) < TOTAL_MAX))
    def _():
        for start in range(0, count, chunk):
            rows = slice(start, start + chunk)
            top, total, acc = running_softmax(
                query_ref[rows, :],
                (other_key_ref, key_ref),
                (other_value_ref, value_ref),
                key_block,
                scale,
            )
            wide = (chunk, head_dim)
            top, total = jnp.broadcast_to(top, wide), jnp.broadcast_to(total, wide)
            write_parts(part_ref, start // group, group, top, total, acc)
        copy = pltpu.make_async_copy(part_ref, out_ref, sems.at[0])
        copy.start()
        copy.wait()


def prefix_parts(query_rows, keys, values, other_keys, other_values, group, scale):
    count, head_dim = query_rows.shape
    positions = keys.shape[0]
    held = pl.BlockSpec(memory_space=pltpu.VMEM)
    limit = pltpu.CompilerParams(vmem_limit_bytes=32 * 2**20)
    key_block = min(256, positions)
    chunk = min(256, count)
    cost = pl.CostEstimate(
        flops=6 * count * positions * head_dim,
        bytes_accessed=4 * positions * head_dim,
        transcendentals=count * positions,
    )
    top, state = pl.pallas_call(
        functools.partial(first_kernel, chunk=chunk, key_block=key_block, scale=scale),
        in_specs=[held] * 3,
        out_specs=[held] * 2,
        out_shape=[
            jax.ShapeDtypeStruct((count, head_dim), jnp.float32),
            jax.ShapeDtypeStruct((count, 2 * head_dim), jnp.float32),
        ],
        compiler_params=limit,
        cost_estimate=cost,
        name="prefix_first",
    )(query_rows, other_keys, other_values)
    shape = (count // group, group + STAT_ROWS, head_dim)
    return pl.pallas_call(
        functools.partial(
            second_kernel, chunk=chunk, key_block=key_block, group=group, scale=scale
        ),
        in_specs=[held] * 7,
        out_specs=pl.BlockSpec(memory_space=pltpu.HBM),
        out_shape=jax.ShapeDtypeStruct(shape, jnp.bfloat16),
        scratch_shapes=[
            pltpu.VMEM(shape, jnp.bfloat16),
            pltpu.SemaphoreType.DMA((count // chunk,)),
        ],
        compiler_params=limit,
        cost_estimate=cost,
        name="prefix_second",
    )(query_rows, keys, values, other_keys, other_values, top, state)


def suffix_kernel(
    length_ref, query_ref, new_key_ref, new_value_ref, key_ref, value_ref,
    mean_ref, top_ref, total_ref, key_held, value_held, sems, *, key_block, group_size, scale,
):
    requests, rows, head_dim = query_ref.shape
    blocks = key_ref.shape[1] // key_block
    pair = 2 if requests % 2 == 0 else 1

    def copies(request, block):
        span = pl.ds(block * key_block, key_block)
        return [
            pltpu.make_async_copy(
                source.at[request, span, :], target.at[request, span, :], sems.at[kind, request, block]
            )
            for kind, (source, target) in enumerate(((key_ref, key_held), (value_ref, value_held)))
        ]

    def filled(start, block):
        longest = length_ref[start]
        for request in range(start + 1, start + pair):
            longest = jnp.maximum(longest, length_ref[request])
        return block * key_block < longest

    def absorb(request, block, top, total, acc):
        span = pl.ds(block * key_block, key_block)
        scores = dot_rows(query_ref[request], key_held[request, span, :]) * scale
        slot = block * key_block + lax.broadcasted_iota(jnp.int32, scores.shape, 1)
        scores = jnp.where(slot < length_ref[request], scores, LOW)
        new_top = jnp.maximum(top, jnp.max(scores, axis=1, keepdims=True))
        weights = jnp.exp2(scores - new_top)
        rescale = jnp.exp2(top - new_top)
        total = total * rescale + jnp.sum(weights, axis=1, keepdims=True)
        acc = acc * rescale + jnp.dot(
            weights.astype(jnp.bfloat16),
            value_held[request, span, :],
            preferred_element_type=jnp.float32,
        )
        return new_top, total, acc

    def keep(request, top, total, acc):
        mean_ref[request] = acc
        top_ref[request] = jnp.broadcast_to(top, (rows, head_dim))
        total_ref[request] = jnp.broadcast_to(total, (rows, head_dim))

    for request in range(requests):
        for copy in copies(request, 0):
            copy.start()
    for block in range(1, blocks):
        for start in range(0, requests, pair):

            @pl.when(filled(start, block))
            def _(start=start, block=block):
                for request in range(start, start + pair):
                    for copy in copies(request, block):
                        copy.start()

    for request in range(requests):
        for copy in copies(request, 0):
            copy.wait()
    states = []
    for request in range(requests):
        count = new_key_ref.shape[1]
        scores = dot_rows(query_ref[request], new_key_ref[request]) * scale
        step = lax.broadcasted_iota(jnp.int32, (rows, count), 0) // group_size
        slot = lax.broadcasted_iota(jnp.int32, (rows, count), 1)
        allowed = step >= slot
        top = jnp.max(jnp.where(allowed, scores, LOW), axis=1, keepdims=True)
        weights = jnp.where(allowed, jnp.exp2(scores - top), 0.0)
        rounded = weights.astype(jnp.bfloat16).astype(jnp.float32)
        values = new_value_ref[request].astype(jnp.float32)
        acc = rounded[:, 0:1] * values[0:1]
        for index in range(1, count):
            acc = acc + rounded[:, index : index + 1] * values[index : index + 1]
        total = jnp.sum(weights, axis=1, keepdims=True)
        states.append(absorb(request, 0, top, total, acc))
    for request in range(requests):
        keep(request, *states[request])

    for block in range(1, blocks):
        for start in range(0, requests, pair):

            @pl.when(filled(start, block))
            def _(start=start, block=block):
                members = range(start, start + pair)
                for request in members:
                    for copy in copies(request, block):
                        copy.wait()
                states = [
                    absorb(
                        request, block, top_ref[request][:, 0:1], total_ref[request][:, 0:1],
                        mean_ref[request],
                    )
                    for request in members
                ]
                for request, state in zip(members, states):
                    keep(request, *state)

    mean_ref[...] = mean_ref[...] / total_ref[...]


def suffix_part(query_rows, keys, values, new_keys, new_values, lengths, group_size, scale):
    requests, rows, head_dim = query_rows.shape
    slots = keys.shape[1]
    key_block = min(2048, slots)
    held = pl.BlockSpec(memory_space=pltpu.VMEM)
    away = pl.BlockSpec(memory_space=pltpu.HBM)
    return pl.pallas_call(
        functools.partial(suffix_kernel, key_block=key_block, group_size=group_size, scale=scale),
        in_specs=[pl.BlockSpec(memory_space=pltpu.SMEM), held, held, held, away, away],
        out_specs=[held] * 3,
        out_shape=[jax.ShapeDtypeStruct((requests, rows, head_dim), jnp.float32)] * 3,
        scratch_shapes=[pltpu.VMEM(keys.shape, keys.dtype)] * 2
        + [pltpu.SemaphoreType.DMA((2, requests, slots // key_block))],
        compiler_params=pltpu.CompilerParams(vmem_limit_bytes=52 * 2**20),
        cost_estimate=pl.CostEstimate(
            flops=4 * requests * rows * slots * head_dim,
            bytes_accessed=4 * requests * slots * head_dim,
            transcendentals=requests * rows * slots,
        ),
        name="suffix_part",
    )(lengths, query_rows, new_keys, new_values, keys, values)


def combine_kernel(part_ref, mean_ref, top_ref, total_ref, out_ref, acc_ref):
    senders, height, head_dim = part_ref.shape
    rows = height - STAT_ROWS
    lines = out_ref.shape[0]
    heads = rows // lines
    stat = jnp.sum(part_ref[:, rows : rows + STAT_ROWS, :].astype(jnp.float32), axis=1)
    stat = stat.T
    own_top = top_ref[...][:, 0:1]
    own_total = total_ref[...][:, 0:1]
    tops, totals = stat[:rows], stat[rows : 2 * rows]
    peak = jnp.maximum(jnp.max(tops, axis=1, keepdims=True), own_top)
    weights = jnp.exp2(tops - peak) * totals
    own = jnp.exp2(own_top - peak) * own_total
    total = jnp.sum(weights, axis=1, keepdims=True) + own
    acc = mean_ref[...] * own
    for sender in range(senders):
        acc = acc + part_ref[sender, :rows, :].astype(jnp.float32) * weights[:, sender : sender + 1]
    acc_ref[...] = acc / total
    for head in range(heads):
        out_ref[:, head * head_dim : (head + 1) * head_dim] = acc_ref[
            pl.ds(head, lines, stride=heads), :
        ].astype(jnp.bfloat16)


def combine(parts, mean, top, total, lines):
    rows, head_dim = mean.shape
    held = pl.BlockSpec(memory_space=pltpu.VMEM)
    return pl.pallas_call(
        combine_kernel,
        in_specs=[held] * 4,
        out_specs=held,
        out_shape=jax.ShapeDtypeStruct((lines, rows // lines * head_dim), jnp.bfloat16),
        scratch_shapes=[pltpu.VMEM((rows, head_dim), jnp.float32)],
        compiler_params=pltpu.CompilerParams(vmem_limit_bytes=16 * 2**20),
        name="combine_parts",
    )(parts, mean, top, total)


def shards(
    queries, prefix_keys, prefix_values, suffix_keys, suffix_values, new_keys, new_values,
    suffix_lengths, out_weight,
):
    owned, steps, row_width = queries.shape
    head_dim = prefix_keys.shape[2]
    group_size = row_width // head_dim
    group = owned * steps * group_size
    scale = head_dim**-0.5 * LOG2E
    everyone = owned * lax.axis_size("seq")
    devices = lax.axis_size("seq")
    sharers = devices // 2
    same_core = [list(range(core, devices, 2)) for core in range(2)]
    swap_cores = [(index, index ^ 1) for index in range(devices)]
    own_rows = lax.optimization_barrier(queries.reshape(group, head_dim))
    keys, values = prefix_keys[:, 0, :], prefix_values[:, 0, :]
    gathered = lax.all_to_all(
        jnp.tile(own_rows, (sharers, 1)), "seq", 0, 0, axis_index_groups=same_core, tiled=True
    )
    other_keys = lax.ppermute(keys, "seq", swap_cores)
    other_values = lax.ppermute(values, "seq", swap_cores)
    mean, top, total = suffix_part(
        own_rows.reshape(owned, steps * group_size, head_dim),
        suffix_keys[:, :, 0, :], suffix_values[:, :, 0, :],
        new_keys[:, :, 0, :], new_values[:, :, 0, :], suffix_lengths, group_size, scale,
    )
    parts = prefix_parts(gathered, keys, values, other_keys, other_values, group, scale)
    parts = lax.all_to_all(parts, "seq", 0, 0, axis_index_groups=same_core, tiled=True)
    attended = combine(
        parts, mean.reshape(group, head_dim), top.reshape(group, head_dim),
        total.reshape(group, head_dim), owned * steps,
    )
    attended = lax.all_to_all(
        jnp.tile(attended, (sharers, 1)), "seq", 0, 0, axis_index_groups=same_core, tiled=True
    )
    other_attended = lax.ppermute(attended, "seq", swap_cores)
    core = lax.axis_index("seq") % 2
    even = jnp.where(core == 0, attended, other_attended)
    odd = jnp.where(core == 0, other_attended, attended)
    attended = jnp.stack(
        [rows.reshape(sharers, owned * steps, row_width) for rows in (even, odd)], axis=1
    ).reshape(everyone * steps, row_width)
    partial = jnp.dot(attended, out_weight, preferred_element_type=jnp.float32)
    columns = out_weight.shape[1]
    heads = lax.axis_size("head")
    partial = partial.astype(jnp.bfloat16).reshape(heads, everyone * steps // heads, columns)
    partial = lax.all_to_all(partial, "head", 0, 0, tiled=True)
    summed = jnp.sum(partial.astype(jnp.float32), axis=0).astype(jnp.bfloat16)
    return summed.reshape(everyone // heads, steps, columns)


def solution(mesh):
    placed = (
        P("seq", None, "head"),
        P("seq", "head", None),
        P("seq", "head", None),
        P("seq", None, "head", None),
        P("seq", None, "head", None),
        P("seq", None, "head", None),
        P("seq", None, "head", None),
        P("seq"),
        P("head", "seq"),
    )
    return jax.shard_map(
        shards, mesh=mesh, in_specs=placed, out_specs=P("head", None, "seq"), check_vma=False
    )
```

```python
import functools

import jax
import jax.numpy as jnp
from jax import lax
from jax.experimental import pallas as pl
from jax.experimental.pallas import tpu as pltpu
from jax.sharding import PartitionSpec as P

LOW = -1.0e30
LOG2E = 1.4426950408889634
STAT_ROWS = 16
ONES_ROWS = 16
TOTAL_MAX = 2.0**100


def dot_rows(left, right):
    return lax.dot_general(
        left, right, (((1,), (1,)), ((), ())), preferred_element_type=jnp.float32
    )


def split_bf16(value):
    high = value.astype(jnp.bfloat16)
    rest = value - high.astype(jnp.float32)
    middle = rest.astype(jnp.bfloat16)
    low = (rest - middle.astype(jnp.float32)).astype(jnp.bfloat16)
    return high, middle, low


def running_softmax(query_rows, key_refs, value_refs, key_block, scale):
    count, head_dim = query_rows.shape

    def advance(key_ref, value_ref):
        def step(index, state):
            top, total, acc = state
            rows = pl.ds(pl.multiple_of(index * key_block, key_block), key_block)
            scores = dot_rows(query_rows, key_ref[rows, :]) * scale
            new_top = jnp.maximum(top, jnp.max(scores, axis=1, keepdims=True))
            weights = jnp.exp2(scores - new_top)
            rescale = jnp.exp2(top - new_top)
            total = total * rescale + jnp.sum(weights, axis=1, keepdims=True)
            acc = acc * rescale + jnp.dot(
                weights.astype(jnp.bfloat16), value_ref[rows, :], preferred_element_type=jnp.float32
            )
            return new_top, total, acc

        return step

    state = (
        jnp.full((count, 1), LOW, jnp.float32),
        jnp.zeros((count, 1), jnp.float32),
        jnp.zeros((count, head_dim), jnp.float32),
    )
    for key_ref, value_ref in zip(key_refs, value_refs):
        state = lax.fori_loop(
            0, key_ref.shape[0] // key_block, advance(key_ref, value_ref), state
        )
    return state


def shifted_softmax(query_rows, key_ref, value_ref, key_block, scale, top, acc):
    ones = jnp.ones((ONES_ROWS, key_block), jnp.bfloat16)
    spans = [slice(start, start + key_block) for start in range(0, key_ref.shape[0], key_block)]

    def score(span):
        return dot_rows(key_ref[span, :], query_rows) * scale

    scores = score(spans[0])
    for index, span in enumerate(spans):
        later = score(spans[index + 1]) if index + 1 < len(spans) else None
        if top is None:
            top = jnp.max(scores, axis=0, keepdims=True)
        weights = jnp.exp2(scores - top).astype(jnp.bfloat16)
        values = jnp.concatenate([value_ref[span, :].T, ones], axis=0)
        part = jnp.dot(values, weights, preferred_element_type=jnp.float32)
        acc = part if acc is None else acc + part
        scores = later
    return top, acc


def first_kernel(query_ref, key_ref, value_ref, top_ref, state_ref, *, key_block, scale):
    top_ref[...], state_ref[...] = shifted_softmax(
        query_ref[...], key_ref, value_ref, key_block, scale, None, None
    )


def stat_tile(stat):
    high, middle, low = split_bf16(stat)
    row = lax.broadcasted_iota(jnp.int32, stat.shape, 0)
    tile = jnp.where(row == 0, high.astype(jnp.float32), 0.0)
    tile = jnp.where(row == 1, middle.astype(jnp.float32), tile)
    tile = jnp.where(row == 2, low.astype(jnp.float32), tile)
    return tile.astype(jnp.bfloat16)


def write_columns(out_ref, first, group, top, total, acc):
    head_dim = acc.shape[0]
    lane = lax.broadcasted_iota(jnp.int32, (STAT_ROWS, head_dim), 1)
    for index in range(acc.shape[1] // head_dim):
        lanes = slice(index * head_dim, (index + 1) * head_dim)
        mean = (acc[:, lanes] / total[:, lanes]).T.astype(jnp.bfloat16)
        tops = jnp.broadcast_to(top[:, lanes], (STAT_ROWS, head_dim))
        totals = jnp.broadcast_to(total[:, lanes], (STAT_ROWS, head_dim))
        stats = (
            jnp.where(lane < group, tops, pltpu.roll(totals, group, 1)),
            jnp.where(lane < group, pltpu.roll(tops, group, 1), totals),
        )
        for side, stat in enumerate(stats):
            place = first + 2 * index + side
            out_ref[place, :group, :] = mean[side * group : (side + 1) * group]
            out_ref[place, group:, :] = stat_tile(stat)


def write_parts(out_ref, first, group, top, total, acc):
    head_dim = acc.shape[1]
    row = lax.broadcasted_iota(jnp.int32, (group, head_dim), 0)
    lane = lax.broadcasted_iota(jnp.int32, (group, head_dim), 1)
    for index in range(acc.shape[0] // group):
        rows = slice(index * group, (index + 1) * group)
        stat = jnp.where(lane == row, top[rows], 0.0)
        stat = jnp.where(lane == row + group, total[rows], stat)
        stat = jnp.broadcast_to(jnp.sum(stat, axis=0, keepdims=True), (STAT_ROWS, head_dim))
        out_ref[first + index, :group, :] = (acc[rows] / total[rows]).astype(jnp.bfloat16)
        out_ref[first + index, group:, :] = stat_tile(stat)


def second_kernel(
    query_ref, key_ref, value_ref, other_key_ref, other_value_ref, top_ref, state_ref, out_ref,
    part_ref, sems, *, chunk, key_block, group, scale,
):
    count, head_dim = query_ref.shape
    owners = chunk // group
    copies = []
    top = top_ref[...]
    _, acc = shifted_softmax(
        query_ref[...], key_ref, value_ref, key_block, scale, top, state_ref[...]
    )
    totals = acc[head_dim : head_dim + 1]
    for start in range(0, count, chunk):
        lanes = slice(start, start + chunk)
        write_columns(
            part_ref, start // group, group, top[:, lanes], totals[:, lanes], acc[:head_dim, lanes]
        )
        span = pl.ds(start // group, owners)
        copy = pltpu.make_async_copy(part_ref.at[span], out_ref.at[span], sems.at[start // chunk])
        copy.start()
        copies.append(copy)
    for copy in copies:
        copy.wait()

    @pl.when(jnp.logical_not(jnp.max(totals) < TOTAL_MAX))
    def _():
        for start in range(0, count, chunk):
            rows = slice(start, start + chunk)
            top, total, acc = running_softmax(
                query_ref[rows, :],
                (other_key_ref, key_ref),
                (other_value_ref, value_ref),
                key_block,
                scale,
            )
            wide = (chunk, head_dim)
            top, total = jnp.broadcast_to(top, wide), jnp.broadcast_to(total, wide)
            write_parts(part_ref, start // group, group, top, total, acc)
        copy = pltpu.make_async_copy(part_ref, out_ref, sems.at[0])
        copy.start()
        copy.wait()


def prefix_parts(query_rows, keys, values, other_keys, other_values, group, scale):
    count, head_dim = query_rows.shape
    positions = keys.shape[0]
    held = pl.BlockSpec(memory_space=pltpu.VMEM)
    limit = pltpu.CompilerParams(vmem_limit_bytes=32 * 2**20)
    key_block = min(256, positions)
    chunk = min(256, count)
    cost = pl.CostEstimate(
        flops=6 * count * positions * head_dim,
        bytes_accessed=4 * positions * head_dim,
        transcendentals=count * positions,
    )
    top, state = pl.pallas_call(
        functools.partial(first_kernel, key_block=key_block, scale=scale),
        in_specs=[held] * 3,
        out_specs=[held] * 2,
        out_shape=[
            jax.ShapeDtypeStruct((1, count), jnp.float32),
            jax.ShapeDtypeStruct((head_dim + ONES_ROWS, count), jnp.float32),
        ],
        compiler_params=limit,
        cost_estimate=cost,
        name="prefix_first",
    )(query_rows, other_keys, other_values)
    shape = (count // group, group + STAT_ROWS, head_dim)
    return pl.pallas_call(
        functools.partial(
            second_kernel, chunk=chunk, key_block=key_block, group=group, scale=scale
        ),
        in_specs=[held] * 7,
        out_specs=pl.BlockSpec(memory_space=pltpu.HBM),
        out_shape=jax.ShapeDtypeStruct(shape, jnp.bfloat16),
        scratch_shapes=[
            pltpu.VMEM(shape, jnp.bfloat16),
            pltpu.SemaphoreType.DMA((count // chunk,)),
        ],
        compiler_params=limit,
        cost_estimate=cost,
        name="prefix_second",
    )(query_rows, keys, values, other_keys, other_values, top, state)


def suffix_kernel(
    length_ref, query_ref, new_key_ref, new_value_ref, key_ref, value_ref,
    mean_ref, top_ref, total_ref, key_held, value_held, sems, *, key_block, group_size, scale,
):
    requests, rows, head_dim = query_ref.shape
    blocks = key_ref.shape[1] // key_block
    pair = 2 if requests % 2 == 0 else 1

    def copies(request, block):
        span = pl.ds(block * key_block, key_block)
        return [
            pltpu.make_async_copy(
                source.at[request, span, :], target.at[request, span, :], sems.at[kind, request, block]
            )
            for kind, (source, target) in enumerate(((key_ref, key_held), (value_ref, value_held)))
        ]

    def filled(start, block):
        longest = length_ref[start]
        for request in range(start + 1, start + pair):
            longest = jnp.maximum(longest, length_ref[request])
        return block * key_block < longest

    def absorb(request, block, top, total, acc):
        span = pl.ds(block * key_block, key_block)
        scores = dot_rows(query_ref[request], key_held[request, span, :]) * scale
        slot = block * key_block + lax.broadcasted_iota(jnp.int32, scores.shape, 1)
        scores = jnp.where(slot < length_ref[request], scores, LOW)
        new_top = jnp.maximum(top, jnp.max(scores, axis=1, keepdims=True))
        weights = jnp.exp2(scores - new_top)
        rescale = jnp.exp2(top - new_top)
        total = total * rescale + jnp.sum(weights, axis=1, keepdims=True)
        acc = acc * rescale + jnp.dot(
            weights.astype(jnp.bfloat16),
            value_held[request, span, :],
            preferred_element_type=jnp.float32,
        )
        return new_top, total, acc

    def keep(request, top, total, acc):
        mean_ref[request] = acc
        top_ref[request] = jnp.broadcast_to(top, (rows, head_dim))
        total_ref[request] = jnp.broadcast_to(total, (rows, head_dim))

    for request in range(requests):
        for copy in copies(request, 0):
            copy.start()
    for block in range(1, blocks):
        for start in range(0, requests, pair):

            @pl.when(filled(start, block))
            def _(start=start, block=block):
                for request in range(start, start + pair):
                    for copy in copies(request, block):
                        copy.start()

    for request in range(requests):
        for copy in copies(request, 0):
            copy.wait()
    states = []
    for request in range(requests):
        count = new_key_ref.shape[1]
        scores = dot_rows(query_ref[request], new_key_ref[request]) * scale
        step = lax.broadcasted_iota(jnp.int32, (rows, count), 0) // group_size
        slot = lax.broadcasted_iota(jnp.int32, (rows, count), 1)
        allowed = step >= slot
        top = jnp.max(jnp.where(allowed, scores, LOW), axis=1, keepdims=True)
        weights = jnp.where(allowed, jnp.exp2(scores - top), 0.0)
        rounded = weights.astype(jnp.bfloat16).astype(jnp.float32)
        values = new_value_ref[request].astype(jnp.float32)
        acc = rounded[:, 0:1] * values[0:1]
        for index in range(1, count):
            acc = acc + rounded[:, index : index + 1] * values[index : index + 1]
        total = jnp.sum(weights, axis=1, keepdims=True)
        states.append(absorb(request, 0, top, total, acc))
    for request in range(requests):
        keep(request, *states[request])

    for block in range(1, blocks):
        for start in range(0, requests, pair):

            @pl.when(filled(start, block))
            def _(start=start, block=block):
                members = range(start, start + pair)
                for request in members:
                    for copy in copies(request, block):
                        copy.wait()
                states = [
                    absorb(
                        request, block, top_ref[request][:, 0:1], total_ref[request][:, 0:1],
                        mean_ref[request],
                    )
                    for request in members
                ]
                for request, state in zip(members, states):
                    keep(request, *state)

    mean_ref[...] = mean_ref[...] / total_ref[...]


def suffix_part(query_rows, keys, values, new_keys, new_values, lengths, group_size, scale):
    requests, rows, head_dim = query_rows.shape
    slots = keys.shape[1]
    key_block = min(2048, slots)
    held = pl.BlockSpec(memory_space=pltpu.VMEM)
    away = pl.BlockSpec(memory_space=pltpu.HBM)
    return pl.pallas_call(
        functools.partial(suffix_kernel, key_block=key_block, group_size=group_size, scale=scale),
        in_specs=[pl.BlockSpec(memory_space=pltpu.SMEM), held, held, held, away, away],
        out_specs=[held] * 3,
        out_shape=[jax.ShapeDtypeStruct((requests, rows, head_dim), jnp.float32)] * 3,
        scratch_shapes=[pltpu.VMEM(keys.shape, keys.dtype)] * 2
        + [pltpu.SemaphoreType.DMA((2, requests, slots // key_block))],
        compiler_params=pltpu.CompilerParams(vmem_limit_bytes=52 * 2**20),
        cost_estimate=pl.CostEstimate(
            flops=4 * requests * rows * slots * head_dim,
            bytes_accessed=4 * requests * slots * head_dim,
            transcendentals=requests * rows * slots,
        ),
        name="suffix_part",
    )(lengths, query_rows, new_keys, new_values, keys, values)


def combine_kernel(part_ref, mean_ref, top_ref, total_ref, out_ref, acc_ref):
    senders, height, head_dim = part_ref.shape
    rows = height - STAT_ROWS
    lines = out_ref.shape[0]
    heads = rows // lines
    stat = jnp.sum(part_ref[:, rows : rows + STAT_ROWS, :].astype(jnp.float32), axis=1)
    stat = stat.T
    own_top = top_ref[...][:, 0:1]
    own_total = total_ref[...][:, 0:1]
    tops, totals = stat[:rows], stat[rows : 2 * rows]
    peak = jnp.maximum(jnp.max(tops, axis=1, keepdims=True), own_top)
    weights = jnp.exp2(tops - peak) * totals
    own = jnp.exp2(own_top - peak) * own_total
    total = jnp.sum(weights, axis=1, keepdims=True) + own
    acc = mean_ref[...] * own
    for sender in range(senders):
        acc = acc + part_ref[sender, :rows, :].astype(jnp.float32) * weights[:, sender : sender + 1]
    acc_ref[...] = acc / total
    for head in range(heads):
        out_ref[:, head * head_dim : (head + 1) * head_dim] = acc_ref[
            pl.ds(head, lines, stride=heads), :
        ].astype(jnp.bfloat16)


def combine(parts, mean, top, total, lines):
    rows, head_dim = mean.shape
    held = pl.BlockSpec(memory_space=pltpu.VMEM)
    return pl.pallas_call(
        combine_kernel,
        in_specs=[held] * 4,
        out_specs=held,
        out_shape=jax.ShapeDtypeStruct((lines, rows // lines * head_dim), jnp.bfloat16),
        scratch_shapes=[pltpu.VMEM((rows, head_dim), jnp.float32)],
        compiler_params=pltpu.CompilerParams(vmem_limit_bytes=16 * 2**20),
        name="combine_parts",
    )(parts, mean, top, total)


def shards(
    queries, prefix_keys, prefix_values, suffix_keys, suffix_values, new_keys, new_values,
    suffix_lengths, out_weight,
):
    owned, steps, row_width = queries.shape
    head_dim = prefix_keys.shape[2]
    group_size = row_width // head_dim
    group = owned * steps * group_size
    scale = head_dim**-0.5 * LOG2E
    everyone = owned * lax.axis_size("seq")
    devices = lax.axis_size("seq")
    sharers = devices // 2
    same_core = [list(range(core, devices, 2)) for core in range(2)]
    swap_cores = [(index, index ^ 1) for index in range(devices)]
    own_rows = lax.optimization_barrier(queries.reshape(group, head_dim))
    keys, values = prefix_keys[:, 0, :], prefix_values[:, 0, :]
    gathered = lax.all_to_all(
        jnp.tile(own_rows, (sharers, 1)), "seq", 0, 0, axis_index_groups=same_core, tiled=True
    )
    other_keys = lax.ppermute(keys, "seq", swap_cores)
    other_values = lax.ppermute(values, "seq", swap_cores)
    mean, top, total = suffix_part(
        own_rows.reshape(owned, steps * group_size, head_dim),
        suffix_keys[:, :, 0, :], suffix_values[:, :, 0, :],
        new_keys[:, :, 0, :], new_values[:, :, 0, :], suffix_lengths, group_size, scale,
    )
    parts = prefix_parts(gathered, keys, values, other_keys, other_values, group, scale)
    parts = lax.all_to_all(parts, "seq", 0, 0, axis_index_groups=same_core, tiled=True)
    attended = combine(
        parts, mean.reshape(group, head_dim), top.reshape(group, head_dim),
        total.reshape(group, head_dim), owned * steps,
    )
    attended = lax.all_to_all(
        jnp.tile(attended, (sharers, 1)), "seq", 0, 0, axis_index_groups=same_core, tiled=True
    )
    other_attended = lax.ppermute(attended, "seq", swap_cores)
    core = lax.axis_index("seq") % 2
    even = jnp.where(core == 0, attended, other_attended)
    odd = jnp.where(core == 0, other_attended, attended)
    attended = jnp.stack(
        [rows.reshape(sharers, owned * steps, row_width) for rows in (even, odd)], axis=1
    ).reshape(everyone * steps, row_width)
    partial = jnp.dot(attended, out_weight, preferred_element_type=jnp.float32)
    columns = out_weight.shape[1]
    heads = lax.axis_size("head")
    partial = partial.astype(jnp.bfloat16).reshape(heads, everyone * steps // heads, columns)
    partial = lax.all_to_all(partial, "head", 0, 0, tiled=True)
    summed = jnp.sum(partial.astype(jnp.float32), axis=0).astype(jnp.bfloat16)
    return summed.reshape(everyone // heads, steps, columns)


def solution(mesh):
    placed = (
        P("seq", None, "head"),
        P("seq", "head", None),
        P("seq", "head", None),
        P("seq", None, "head", None),
        P("seq", None, "head", None),
        P("seq", None, "head", None),
        P("seq", None, "head", None),
        P("seq"),
        P("head", "seq"),
    )
    return jax.shard_map(
        shards, mesh=mesh, in_specs=placed, out_specs=P("head", None, "seq"), check_vma=False
    )
```

```python
import functools

import jax
import jax.numpy as jnp
from jax import lax
from jax.experimental import pallas as pl
from jax.experimental.pallas import tpu as pltpu
from jax.sharding import PartitionSpec as P

LOW = -1.0e30
LOG2E = 1.4426950408889634
STAT_ROWS = 16
ONES_ROWS = 16
TOTAL_MAX = 2.0**100


def dot_rows(left, right):
    return lax.dot_general(
        left, right, (((1,), (1,)), ((), ())), preferred_element_type=jnp.float32
    )


def split_bf16(value):
    high = value.astype(jnp.bfloat16)
    rest = value - high.astype(jnp.float32)
    middle = rest.astype(jnp.bfloat16)
    low = (rest - middle.astype(jnp.float32)).astype(jnp.bfloat16)
    return high, middle, low


def running_softmax(query_rows, key_refs, value_refs, key_block, scale):
    count, head_dim = query_rows.shape

    def advance(key_ref, value_ref):
        def step(index, state):
            top, total, acc = state
            rows = pl.ds(pl.multiple_of(index * key_block, key_block), key_block)
            scores = dot_rows(query_rows, key_ref[rows, :]) * scale
            new_top = jnp.maximum(top, jnp.max(scores, axis=1, keepdims=True))
            weights = jnp.exp2(scores - new_top)
            rescale = jnp.exp2(top - new_top)
            total = total * rescale + jnp.sum(weights, axis=1, keepdims=True)
            acc = acc * rescale + jnp.dot(
                weights.astype(jnp.bfloat16), value_ref[rows, :], preferred_element_type=jnp.float32
            )
            return new_top, total, acc

        return step

    state = (
        jnp.full((count, 1), LOW, jnp.float32),
        jnp.zeros((count, 1), jnp.float32),
        jnp.zeros((count, head_dim), jnp.float32),
    )
    for key_ref, value_ref in zip(key_refs, value_refs):
        state = lax.fori_loop(
            0, key_ref.shape[0] // key_block, advance(key_ref, value_ref), state
        )
    return state


def shifted_softmax(query_rows, key_ref, value_ref, key_block, scale, top, acc):
    ones = jnp.ones((ONES_ROWS, key_block), jnp.bfloat16)
    spans = [slice(start, start + key_block) for start in range(0, key_ref.shape[0], key_block)]

    def score(span):
        return dot_rows(key_ref[span, :], query_rows) * scale

    scores = score(spans[0])
    for index, span in enumerate(spans):
        later = score(spans[index + 1]) if index + 1 < len(spans) else None
        if top is None:
            top = jnp.max(scores, axis=0, keepdims=True)
        weights = jnp.exp2(scores - top).astype(jnp.bfloat16)
        values = jnp.concatenate([value_ref[span, :].T, ones], axis=0)
        part = jnp.dot(values, weights, preferred_element_type=jnp.float32)
        acc = part if acc is None else acc + part
        scores = later
    return top, acc


def first_kernel(query_ref, key_ref, value_ref, top_ref, state_ref, *, key_block, scale):
    top_ref[...], state_ref[...] = shifted_softmax(
        query_ref[...], key_ref, value_ref, key_block, scale, None, None
    )


def stat_tile(stat):
    high, middle, low = split_bf16(stat)
    row = lax.broadcasted_iota(jnp.int32, stat.shape, 0)
    tile = jnp.where(row == 0, high.astype(jnp.float32), 0.0)
    tile = jnp.where(row == 1, middle.astype(jnp.float32), tile)
    tile = jnp.where(row == 2, low.astype(jnp.float32), tile)
    return tile.astype(jnp.bfloat16)


def write_columns(out_ref, first, group, top, total, acc):
    head_dim = acc.shape[0]
    inverse = 1.0 / total
    lane = lax.broadcasted_iota(jnp.int32, (STAT_ROWS, head_dim), 1)
    for index in range(acc.shape[1] // head_dim):
        lanes = slice(index * head_dim, (index + 1) * head_dim)
        mean = (acc[:, lanes] * inverse[:, lanes]).T.astype(jnp.bfloat16)
        tops = jnp.broadcast_to(top[:, lanes], (STAT_ROWS, head_dim))
        totals = jnp.broadcast_to(total[:, lanes], (STAT_ROWS, head_dim))
        stats = (
            jnp.where(lane < group, tops, pltpu.roll(totals, group, 1)),
            jnp.where(lane < group, pltpu.roll(tops, group, 1), totals),
        )
        for side, stat in enumerate(stats):
            place = first + 2 * index + side
            out_ref[place, :group, :] = mean[side * group : (side + 1) * group]
            out_ref[place, group:, :] = stat_tile(stat)


def write_parts(out_ref, first, group, top, total, acc):
    head_dim = acc.shape[1]
    row = lax.broadcasted_iota(jnp.int32, (group, head_dim), 0)
    lane = lax.broadcasted_iota(jnp.int32, (group, head_dim), 1)
    for index in range(acc.shape[0] // group):
        rows = slice(index * group, (index + 1) * group)
        stat = jnp.where(lane == row, top[rows], 0.0)
        stat = jnp.where(lane == row + group, total[rows], stat)
        stat = jnp.broadcast_to(jnp.sum(stat, axis=0, keepdims=True), (STAT_ROWS, head_dim))
        out_ref[first + index, :group, :] = (acc[rows] / total[rows]).astype(jnp.bfloat16)
        out_ref[first + index, group:, :] = stat_tile(stat)


def second_kernel(
    query_ref, key_ref, value_ref, other_key_ref, other_value_ref, top_ref, state_ref, out_ref,
    part_ref, sems, *, chunk, key_block, group, scale,
):
    count, head_dim = query_ref.shape
    owners = chunk // group
    copies = []
    top = top_ref[...]
    _, acc = shifted_softmax(
        query_ref[...], key_ref, value_ref, key_block, scale, top, state_ref[...]
    )
    totals = acc[head_dim : head_dim + 1]
    for start in range(0, count, chunk):
        lanes = slice(start, start + chunk)
        write_columns(
            part_ref, start // group, group, top[:, lanes], totals[:, lanes], acc[:head_dim, lanes]
        )
        span = pl.ds(start // group, owners)
        copy = pltpu.make_async_copy(part_ref.at[span], out_ref.at[span], sems.at[start // chunk])
        copy.start()
        copies.append(copy)
    for copy in copies:
        copy.wait()

    @pl.when(jnp.logical_not(jnp.max(totals) < TOTAL_MAX))
    def _():
        for start in range(0, count, chunk):
            rows = slice(start, start + chunk)
            top, total, acc = running_softmax(
                query_ref[rows, :],
                (other_key_ref, key_ref),
                (other_value_ref, value_ref),
                key_block,
                scale,
            )
            wide = (chunk, head_dim)
            top, total = jnp.broadcast_to(top, wide), jnp.broadcast_to(total, wide)
            write_parts(part_ref, start // group, group, top, total, acc)
        copy = pltpu.make_async_copy(part_ref, out_ref, sems.at[0])
        copy.start()
        copy.wait()


def prefix_parts(query_rows, keys, values, other_keys, other_values, group, scale):
    count, head_dim = query_rows.shape
    positions = keys.shape[0]
    held = pl.BlockSpec(memory_space=pltpu.VMEM)
    limit = pltpu.CompilerParams(vmem_limit_bytes=32 * 2**20)
    key_block = min(256, positions)
    chunk = min(512, count)
    cost = pl.CostEstimate(
        flops=6 * count * positions * head_dim,
        bytes_accessed=4 * positions * head_dim,
        transcendentals=count * positions,
    )
    top, state = pl.pallas_call(
        functools.partial(first_kernel, key_block=key_block, scale=scale),
        in_specs=[held] * 3,
        out_specs=[held] * 2,
        out_shape=[
            jax.ShapeDtypeStruct((1, count), jnp.float32),
            jax.ShapeDtypeStruct((head_dim + ONES_ROWS, count), jnp.float32),
        ],
        compiler_params=limit,
        cost_estimate=cost,
        name="prefix_first",
    )(query_rows, other_keys, other_values)
    shape = (count // group, group + STAT_ROWS, head_dim)
    return pl.pallas_call(
        functools.partial(
            second_kernel, chunk=chunk, key_block=key_block, group=group, scale=scale
        ),
        in_specs=[held] * 7,
        out_specs=pl.BlockSpec(memory_space=pltpu.HBM),
        out_shape=jax.ShapeDtypeStruct(shape, jnp.bfloat16),
        scratch_shapes=[
            pltpu.VMEM(shape, jnp.bfloat16),
            pltpu.SemaphoreType.DMA((count // chunk,)),
        ],
        compiler_params=limit,
        cost_estimate=cost,
        name="prefix_second",
    )(query_rows, keys, values, other_keys, other_values, top, state)


def suffix_kernel(
    length_ref, query_ref, new_key_ref, new_value_ref, key_ref, value_ref,
    mean_ref, top_ref, total_ref, key_held, value_held, sems, *, key_block, group_size, scale,
):
    requests, rows, head_dim = query_ref.shape
    blocks = key_ref.shape[1] // key_block
    pair = 2 if requests % 2 == 0 else 1

    def copies(request, block):
        span = pl.ds(block * key_block, key_block)
        return [
            pltpu.make_async_copy(
                source.at[request, span, :], target.at[request, span, :], sems.at[kind, request, block]
            )
            for kind, (source, target) in enumerate(((key_ref, key_held), (value_ref, value_held)))
        ]

    def filled(start, block):
        longest = length_ref[start]
        for request in range(start + 1, start + pair):
            longest = jnp.maximum(longest, length_ref[request])
        return block * key_block < longest

    def absorb(request, block, top, total, acc):
        span = pl.ds(block * key_block, key_block)
        scores = dot_rows(query_ref[request], key_held[request, span, :]) * scale
        slot = block * key_block + lax.broadcasted_iota(jnp.int32, scores.shape, 1)
        scores = jnp.where(slot < length_ref[request], scores, LOW)
        new_top = jnp.maximum(top, jnp.max(scores, axis=1, keepdims=True))
        weights = jnp.exp2(scores - new_top)
        rescale = jnp.exp2(top - new_top)
        total = total * rescale + jnp.sum(weights, axis=1, keepdims=True)
        acc = acc * rescale + jnp.dot(
            weights.astype(jnp.bfloat16),
            value_held[request, span, :],
            preferred_element_type=jnp.float32,
        )
        return new_top, total, acc

    def keep(request, top, total, acc):
        mean_ref[request] = acc
        top_ref[request] = jnp.broadcast_to(top, (rows, head_dim))
        total_ref[request] = jnp.broadcast_to(total, (rows, head_dim))

    for request in range(requests):
        for copy in copies(request, 0):
            copy.start()
    for block in range(1, blocks):
        for start in range(0, requests, pair):

            @pl.when(filled(start, block))
            def _(start=start, block=block):
                for request in range(start, start + pair):
                    for copy in copies(request, block):
                        copy.start()

    for request in range(requests):
        for copy in copies(request, 0):
            copy.wait()
    states = []
    for request in range(requests):
        count = new_key_ref.shape[1]
        scores = dot_rows(query_ref[request], new_key_ref[request]) * scale
        step = lax.broadcasted_iota(jnp.int32, (rows, count), 0) // group_size
        slot = lax.broadcasted_iota(jnp.int32, (rows, count), 1)
        allowed = step >= slot
        top = jnp.max(jnp.where(allowed, scores, LOW), axis=1, keepdims=True)
        weights = jnp.where(allowed, jnp.exp2(scores - top), 0.0)
        rounded = weights.astype(jnp.bfloat16).astype(jnp.float32)
        values = new_value_ref[request].astype(jnp.float32)
        acc = rounded[:, 0:1] * values[0:1]
        for index in range(1, count):
            acc = acc + rounded[:, index : index + 1] * values[index : index + 1]
        total = jnp.sum(weights, axis=1, keepdims=True)
        states.append(absorb(request, 0, top, total, acc))
    for request in range(requests):
        keep(request, *states[request])

    for block in range(1, blocks):
        for start in range(0, requests, pair):

            @pl.when(filled(start, block))
            def _(start=start, block=block):
                members = range(start, start + pair)
                for request in members:
                    for copy in copies(request, block):
                        copy.wait()
                states = [
                    absorb(
                        request, block, top_ref[request][:, 0:1], total_ref[request][:, 0:1],
                        mean_ref[request],
                    )
                    for request in members
                ]
                for request, state in zip(members, states):
                    keep(request, *state)

    mean_ref[...] = mean_ref[...] / total_ref[...]


def suffix_part(query_rows, keys, values, new_keys, new_values, lengths, group_size, scale):
    requests, rows, head_dim = query_rows.shape
    slots = keys.shape[1]
    key_block = min(2048, slots)
    held = pl.BlockSpec(memory_space=pltpu.VMEM)
    away = pl.BlockSpec(memory_space=pltpu.HBM)
    return pl.pallas_call(
        functools.partial(suffix_kernel, key_block=key_block, group_size=group_size, scale=scale),
        in_specs=[pl.BlockSpec(memory_space=pltpu.SMEM), held, held, held, away, away],
        out_specs=[held] * 3,
        out_shape=[jax.ShapeDtypeStruct((requests, rows, head_dim), jnp.float32)] * 3,
        scratch_shapes=[pltpu.VMEM(keys.shape, keys.dtype)] * 2
        + [pltpu.SemaphoreType.DMA((2, requests, slots // key_block))],
        compiler_params=pltpu.CompilerParams(vmem_limit_bytes=52 * 2**20),
        cost_estimate=pl.CostEstimate(
            flops=4 * requests * rows * slots * head_dim,
            bytes_accessed=4 * requests * slots * head_dim,
            transcendentals=requests * rows * slots,
        ),
        name="suffix_part",
    )(lengths, query_rows, new_keys, new_values, keys, values)


def combine_kernel(part_ref, mean_ref, top_ref, total_ref, out_ref, acc_ref):
    senders, height, head_dim = part_ref.shape
    rows = height - STAT_ROWS
    lines = out_ref.shape[0]
    heads = rows // lines
    stat = jnp.sum(part_ref[:, rows : rows + STAT_ROWS, :].astype(jnp.float32), axis=1)
    stat = stat.T
    own_top = top_ref[...][:, 0:1]
    own_total = total_ref[...][:, 0:1]
    tops, totals = stat[:rows], stat[rows : 2 * rows]
    peak = jnp.maximum(jnp.max(tops, axis=1, keepdims=True), own_top)
    weights = jnp.exp2(tops - peak) * totals
    own = jnp.exp2(own_top - peak) * own_total
    total = jnp.sum(weights, axis=1, keepdims=True) + own
    acc = mean_ref[...] * own
    for sender in range(senders):
        acc = acc + part_ref[sender, :rows, :].astype(jnp.float32) * weights[:, sender : sender + 1]
    acc_ref[...] = acc * (1.0 / total)
    for head in range(heads):
        out_ref[:, head * head_dim : (head + 1) * head_dim] = acc_ref[
            pl.ds(head, lines, stride=heads), :
        ].astype(jnp.bfloat16)


def combine(parts, mean, top, total, lines):
    rows, head_dim = mean.shape
    held = pl.BlockSpec(memory_space=pltpu.VMEM)
    return pl.pallas_call(
        combine_kernel,
        in_specs=[held] * 4,
        out_specs=held,
        out_shape=jax.ShapeDtypeStruct((lines, rows // lines * head_dim), jnp.bfloat16),
        scratch_shapes=[pltpu.VMEM((rows, head_dim), jnp.float32)],
        compiler_params=pltpu.CompilerParams(vmem_limit_bytes=16 * 2**20),
        name="combine_parts",
    )(parts, mean, top, total)


def head_sum_kernel(part_ref, out_ref):
    total = part_ref[0].astype(jnp.float32)
    for head in range(1, part_ref.shape[0]):
        total = total + part_ref[head].astype(jnp.float32)
    steps = out_ref.shape[1]
    for request in range(out_ref.shape[0]):
        rows = total[request * steps : (request + 1) * steps]
        out_ref[request] = rows.astype(jnp.bfloat16)


def head_sum(parts, steps):
    _, rows, columns = parts.shape
    held = pl.BlockSpec(memory_space=pltpu.VMEM)
    return pl.pallas_call(
        head_sum_kernel,
        in_specs=[held],
        out_specs=held,
        out_shape=jax.ShapeDtypeStruct((rows // steps, steps, columns), jnp.bfloat16),
        compiler_params=pltpu.CompilerParams(vmem_limit_bytes=16 * 2**20),
        name="head_sum",
    )(parts)


def shards(
    queries, prefix_keys, prefix_values, suffix_keys, suffix_values, new_keys, new_values,
    suffix_lengths, out_weight,
):
    owned, steps, row_width = queries.shape
    head_dim = prefix_keys.shape[2]
    group_size = row_width // head_dim
    group = owned * steps * group_size
    scale = head_dim**-0.5 * LOG2E
    everyone = owned * lax.axis_size("seq")
    devices = lax.axis_size("seq")
    sharers = devices // 2
    same_core = [list(range(core, devices, 2)) for core in range(2)]
    swap_cores = [(index, index ^ 1) for index in range(devices)]
    own_rows = lax.optimization_barrier(queries.reshape(group, head_dim))
    keys, values = prefix_keys[:, 0, :], prefix_values[:, 0, :]
    gathered = lax.all_to_all(
        jnp.tile(own_rows, (sharers, 1)), "seq", 0, 0, axis_index_groups=same_core, tiled=True
    )
    other_keys = lax.ppermute(keys, "seq", swap_cores)
    other_values = lax.ppermute(values, "seq", swap_cores)
    mean, top, total = suffix_part(
        own_rows.reshape(owned, steps * group_size, head_dim),
        suffix_keys[:, :, 0, :], suffix_values[:, :, 0, :],
        new_keys[:, :, 0, :], new_values[:, :, 0, :], suffix_lengths, group_size, scale,
    )
    parts = prefix_parts(gathered, keys, values, other_keys, other_values, group, scale)
    parts = lax.all_to_all(parts, "seq", 0, 0, axis_index_groups=same_core, tiled=True)
    attended = combine(
        parts, mean.reshape(group, head_dim), top.reshape(group, head_dim),
        total.reshape(group, head_dim), owned * steps,
    )
    attended = lax.all_to_all(
        jnp.tile(attended, (sharers, 1)), "seq", 0, 0, axis_index_groups=same_core, tiled=True
    )
    other_attended = lax.ppermute(attended, "seq", swap_cores)
    core = lax.axis_index("seq") % 2
    even = jnp.where(core == 0, attended, other_attended)
    odd = jnp.where(core == 0, other_attended, attended)
    attended = jnp.stack(
        [rows.reshape(sharers, owned * steps, row_width) for rows in (even, odd)], axis=1
    ).reshape(everyone * steps, row_width)
    partial = jnp.dot(attended, out_weight, preferred_element_type=jnp.float32)
    columns = out_weight.shape[1]
    heads = lax.axis_size("head")
    partial = partial.astype(jnp.bfloat16).reshape(heads, everyone * steps // heads, columns)
    partial = lax.all_to_all(partial, "head", 0, 0, tiled=True)
    return head_sum(partial, steps)


def solution(mesh):
    placed = (
        P("seq", None, "head"),
        P("seq", "head", None),
        P("seq", "head", None),
        P("seq", None, "head", None),
        P("seq", None, "head", None),
        P("seq", None, "head", None),
        P("seq", None, "head", None),
        P("seq"),
        P("head", "seq"),
    )
    return jax.shard_map(
        shards, mesh=mesh, in_specs=placed, out_specs=P("head", None, "seq"), check_vma=False
    )
```

```python
import functools

import jax
import jax.numpy as jnp
from jax import lax
from jax.experimental import pallas as pl
from jax.experimental.pallas import tpu as pltpu
from jax.sharding import PartitionSpec as P

LOW = -1.0e30
LOG2E = 1.4426950408889634
STAT_ROWS = 16
ONES_ROWS = 16
TOTAL_MAX = 2.0**100


def dot_rows(left, right):
    return lax.dot_general(
        left, right, (((1,), (1,)), ((), ())), preferred_element_type=jnp.float32
    )


def split_bf16(value):
    high = value.astype(jnp.bfloat16)
    rest = value - high.astype(jnp.float32)
    middle = rest.astype(jnp.bfloat16)
    low = (rest - middle.astype(jnp.float32)).astype(jnp.bfloat16)
    return high, middle, low


def running_softmax(query_rows, key_refs, value_refs, key_block, scale):
    count, head_dim = query_rows.shape

    def advance(key_ref, value_ref):
        def step(index, state):
            top, total, acc = state
            rows = pl.ds(pl.multiple_of(index * key_block, key_block), key_block)
            scores = dot_rows(query_rows, key_ref[rows, :]) * scale
            new_top = jnp.maximum(top, jnp.max(scores, axis=1, keepdims=True))
            weights = jnp.exp2(scores - new_top)
            rescale = jnp.exp2(top - new_top)
            total = total * rescale + jnp.sum(weights, axis=1, keepdims=True)
            acc = acc * rescale + jnp.dot(
                weights.astype(jnp.bfloat16), value_ref[rows, :], preferred_element_type=jnp.float32
            )
            return new_top, total, acc

        return step

    state = (
        jnp.full((count, 1), LOW, jnp.float32),
        jnp.zeros((count, 1), jnp.float32),
        jnp.zeros((count, head_dim), jnp.float32),
    )
    for key_ref, value_ref in zip(key_refs, value_refs):
        state = lax.fori_loop(
            0, key_ref.shape[0] // key_block, advance(key_ref, value_ref), state
        )
    return state


def shifted_softmax(query_rows, key_ref, value_ref, key_block, scale, top, acc):
    ones = jnp.ones((ONES_ROWS, key_block), jnp.bfloat16)
    spans = [slice(start, start + key_block) for start in range(0, key_ref.shape[0], key_block)]

    def score(span):
        return dot_rows(key_ref[span, :], query_rows) * scale

    scores = score(spans[0])
    for index, span in enumerate(spans):
        later = score(spans[index + 1]) if index + 1 < len(spans) else None
        if top is None:
            top = jnp.max(scores, axis=0, keepdims=True)
        weights = jnp.exp2(scores - top).astype(jnp.bfloat16)
        values = jnp.concatenate([value_ref[span, :].T, ones], axis=0)
        part = jnp.dot(values, weights, preferred_element_type=jnp.float32)
        acc = part if acc is None else acc + part
        scores = later
    return top, acc


def first_kernel(query_ref, key_ref, value_ref, top_ref, state_ref, *, key_block, scale):
    top_ref[...], state_ref[...] = shifted_softmax(
        query_ref[...], key_ref, value_ref, key_block, scale, None, None
    )


def stat_tile(stat):
    high, middle, low = split_bf16(stat)
    row = lax.broadcasted_iota(jnp.int32, stat.shape, 0)
    tile = jnp.where(row == 0, high.astype(jnp.float32), 0.0)
    tile = jnp.where(row == 1, middle.astype(jnp.float32), tile)
    tile = jnp.where(row == 2, low.astype(jnp.float32), tile)
    return tile.astype(jnp.bfloat16)


def write_columns(out_ref, first, group, top, total, acc):
    head_dim = acc.shape[0]
    inverse = 1.0 / total
    lane = lax.broadcasted_iota(jnp.int32, (STAT_ROWS, head_dim), 1)
    for index in range(acc.shape[1] // head_dim):
        lanes = slice(index * head_dim, (index + 1) * head_dim)
        mean = (acc[:, lanes] * inverse[:, lanes]).T.astype(jnp.bfloat16)
        tops = jnp.broadcast_to(top[:, lanes], (STAT_ROWS, head_dim))
        totals = jnp.broadcast_to(total[:, lanes], (STAT_ROWS, head_dim))
        stats = (
            jnp.where(lane < group, tops, pltpu.roll(totals, group, 1)),
            jnp.where(lane < group, pltpu.roll(tops, group, 1), totals),
        )
        for side, stat in enumerate(stats):
            place = first + 2 * index + side
            out_ref[place, :group, :] = mean[side * group : (side + 1) * group]
            out_ref[place, group:, :] = stat_tile(stat)


def write_parts(out_ref, first, group, top, total, acc):
    head_dim = acc.shape[1]
    row = lax.broadcasted_iota(jnp.int32, (group, head_dim), 0)
    lane = lax.broadcasted_iota(jnp.int32, (group, head_dim), 1)
    for index in range(acc.shape[0] // group):
        rows = slice(index * group, (index + 1) * group)
        stat = jnp.where(lane == row, top[rows], 0.0)
        stat = jnp.where(lane == row + group, total[rows], stat)
        stat = jnp.broadcast_to(jnp.sum(stat, axis=0, keepdims=True), (STAT_ROWS, head_dim))
        out_ref[first + index, :group, :] = (acc[rows] / total[rows]).astype(jnp.bfloat16)
        out_ref[first + index, group:, :] = stat_tile(stat)


def second_kernel(
    query_ref, key_ref, value_ref, other_key_ref, other_value_ref, top_ref, state_ref, out_ref,
    part_ref, sems, *, chunk, key_block, group, scale,
):
    count, head_dim = query_ref.shape
    owners = chunk // group
    copies = []
    top = top_ref[...]
    _, acc = shifted_softmax(
        query_ref[...], key_ref, value_ref, key_block, scale, top, state_ref[...]
    )
    totals = acc[head_dim : head_dim + 1]
    for start in range(0, count, chunk):
        lanes = slice(start, start + chunk)
        write_columns(
            part_ref, start // group, group, top[:, lanes], totals[:, lanes], acc[:head_dim, lanes]
        )
        span = pl.ds(start // group, owners)
        copy = pltpu.make_async_copy(part_ref.at[span], out_ref.at[span], sems.at[start // chunk])
        copy.start()
        copies.append(copy)
    for copy in copies:
        copy.wait()

    @pl.when(jnp.logical_not(jnp.max(totals) < TOTAL_MAX))
    def _():
        for start in range(0, count, chunk):
            rows = slice(start, start + chunk)
            top, total, acc = running_softmax(
                query_ref[rows, :],
                (other_key_ref, key_ref),
                (other_value_ref, value_ref),
                key_block,
                scale,
            )
            wide = (chunk, head_dim)
            top, total = jnp.broadcast_to(top, wide), jnp.broadcast_to(total, wide)
            write_parts(part_ref, start // group, group, top, total, acc)
        copy = pltpu.make_async_copy(part_ref, out_ref, sems.at[0])
        copy.start()
        copy.wait()


def prefix_parts(query_rows, keys, values, other_keys, other_values, group, scale):
    count, head_dim = query_rows.shape
    positions = keys.shape[0]
    held = pl.BlockSpec(memory_space=pltpu.VMEM)
    limit = pltpu.CompilerParams(vmem_limit_bytes=32 * 2**20)
    key_block = min(256, positions)
    chunk = min(512, count)
    cost = pl.CostEstimate(
        flops=6 * count * positions * head_dim,
        bytes_accessed=4 * positions * head_dim,
        transcendentals=count * positions,
    )
    top, state = pl.pallas_call(
        functools.partial(first_kernel, key_block=key_block, scale=scale),
        in_specs=[held] * 3,
        out_specs=[held] * 2,
        out_shape=[
            jax.ShapeDtypeStruct((1, count), jnp.float32),
            jax.ShapeDtypeStruct((head_dim + ONES_ROWS, count), jnp.float32),
        ],
        compiler_params=limit,
        cost_estimate=cost,
        name="prefix_first",
    )(query_rows, other_keys, other_values)
    shape = (count // group, group + STAT_ROWS, head_dim)
    return pl.pallas_call(
        functools.partial(
            second_kernel, chunk=chunk, key_block=key_block, group=group, scale=scale
        ),
        in_specs=[held] * 7,
        out_specs=pl.BlockSpec(memory_space=pltpu.HBM),
        out_shape=jax.ShapeDtypeStruct(shape, jnp.bfloat16),
        scratch_shapes=[
            pltpu.VMEM(shape, jnp.bfloat16),
            pltpu.SemaphoreType.DMA((count // chunk,)),
        ],
        compiler_params=limit,
        cost_estimate=cost,
        name="prefix_second",
    )(query_rows, keys, values, other_keys, other_values, top, state)


def suffix_kernel(
    length_ref, query_ref, new_key_ref, new_value_ref, key_ref, value_ref,
    mean_ref, top_ref, total_ref, key_held, value_held, sems, *, key_block, group_size, scale,
):
    requests, rows, head_dim = query_ref.shape
    blocks = key_ref.shape[1] // key_block
    pair = 2 if requests % 2 == 0 else 1

    def copies(request, block):
        span = pl.ds(block * key_block, key_block)
        return [
            pltpu.make_async_copy(
                source.at[request, span, :], target.at[request, span, :], sems.at[kind, request, block]
            )
            for kind, (source, target) in enumerate(((key_ref, key_held), (value_ref, value_held)))
        ]

    def filled(start, block):
        longest = length_ref[start]
        for request in range(start + 1, start + pair):
            longest = jnp.maximum(longest, length_ref[request])
        return block * key_block < longest

    def absorb(request, block, top, total, acc):
        span = pl.ds(block * key_block, key_block)
        scores = dot_rows(query_ref[request], key_held[request, span, :]) * scale
        slot = block * key_block + lax.broadcasted_iota(jnp.int32, scores.shape, 1)
        scores = jnp.where(slot < length_ref[request], scores, LOW)
        new_top = jnp.maximum(top, jnp.max(scores, axis=1, keepdims=True))
        weights = jnp.exp2(scores - new_top)
        rescale = jnp.exp2(top - new_top)
        total = total * rescale + jnp.sum(weights, axis=1, keepdims=True)
        acc = acc * rescale + jnp.dot(
            weights.astype(jnp.bfloat16),
            value_held[request, span, :],
            preferred_element_type=jnp.float32,
        )
        return new_top, total, acc

    def keep(request, top, total, acc):
        mean_ref[request] = acc
        top_ref[request] = jnp.broadcast_to(top, (rows, head_dim))
        total_ref[request] = jnp.broadcast_to(total, (rows, head_dim))

    for request in range(requests):
        for copy in copies(request, 0):
            copy.start()
    for block in range(1, blocks):
        for start in range(0, requests, pair):

            @pl.when(filled(start, block))
            def _(start=start, block=block):
                for request in range(start, start + pair):
                    for copy in copies(request, block):
                        copy.start()

    for request in range(requests):
        for copy in copies(request, 0):
            copy.wait()
    states = []
    for request in range(requests):
        count = new_key_ref.shape[1]
        scores = dot_rows(query_ref[request], new_key_ref[request]) * scale
        step = lax.broadcasted_iota(jnp.int32, (rows, count), 0) // group_size
        slot = lax.broadcasted_iota(jnp.int32, (rows, count), 1)
        allowed = step >= slot
        top = jnp.max(jnp.where(allowed, scores, LOW), axis=1, keepdims=True)
        weights = jnp.where(allowed, jnp.exp2(scores - top), 0.0)
        rounded = weights.astype(jnp.bfloat16).astype(jnp.float32)
        values = new_value_ref[request].astype(jnp.float32)
        acc = rounded[:, 0:1] * values[0:1]
        for index in range(1, count):
            acc = acc + rounded[:, index : index + 1] * values[index : index + 1]
        total = jnp.sum(weights, axis=1, keepdims=True)
        states.append(absorb(request, 0, top, total, acc))
    for request in range(requests):
        keep(request, *states[request])

    for block in range(1, blocks):
        for start in range(0, requests, pair):

            @pl.when(filled(start, block))
            def _(start=start, block=block):
                members = range(start, start + pair)
                for request in members:
                    for copy in copies(request, block):
                        copy.wait()
                states = [
                    absorb(
                        request, block, top_ref[request][:, 0:1], total_ref[request][:, 0:1],
                        mean_ref[request],
                    )
                    for request in members
                ]
                for request, state in zip(members, states):
                    keep(request, *state)

    mean_ref[...] = mean_ref[...] / total_ref[...]


def suffix_part(query_rows, keys, values, new_keys, new_values, lengths, group_size, scale):
    requests, rows, head_dim = query_rows.shape
    slots = keys.shape[1]
    key_block = min(2048, slots)
    held = pl.BlockSpec(memory_space=pltpu.VMEM)
    away = pl.BlockSpec(memory_space=pltpu.HBM)
    return pl.pallas_call(
        functools.partial(suffix_kernel, key_block=key_block, group_size=group_size, scale=scale),
        in_specs=[pl.BlockSpec(memory_space=pltpu.SMEM), held, held, held, away, away],
        out_specs=[held] * 3,
        out_shape=[jax.ShapeDtypeStruct((requests, rows, head_dim), jnp.float32)] * 3,
        scratch_shapes=[pltpu.VMEM(keys.shape, keys.dtype)] * 2
        + [pltpu.SemaphoreType.DMA((2, requests, slots // key_block))],
        compiler_params=pltpu.CompilerParams(vmem_limit_bytes=52 * 2**20),
        cost_estimate=pl.CostEstimate(
            flops=4 * requests * rows * slots * head_dim,
            bytes_accessed=4 * requests * slots * head_dim,
            transcendentals=requests * rows * slots,
        ),
        name="suffix_part",
    )(lengths, query_rows, new_keys, new_values, keys, values)


def combine_kernel(part_ref, mean_ref, top_ref, total_ref, out_ref, acc_ref):
    senders, height, head_dim = part_ref.shape
    rows = height - STAT_ROWS
    lines = out_ref.shape[1]
    heads = rows // lines
    stat = jnp.sum(part_ref[:, rows : rows + STAT_ROWS, :].astype(jnp.float32), axis=1)
    stat = stat.T
    own_top = top_ref[...][:, 0:1]
    own_total = total_ref[...][:, 0:1]
    tops, totals = stat[:rows], stat[rows : 2 * rows]
    peak = jnp.maximum(jnp.max(tops, axis=1, keepdims=True), own_top)
    weights = jnp.exp2(tops - peak) * totals
    own = jnp.exp2(own_top - peak) * own_total
    total = jnp.sum(weights, axis=1, keepdims=True) + own
    acc = mean_ref[...] * own
    for sender in range(senders):
        acc = acc + part_ref[sender, :rows, :].astype(jnp.float32) * weights[:, sender : sender + 1]
    acc_ref[...] = acc * (1.0 / total)
    for head in range(heads):
        part = acc_ref[pl.ds(head, lines, stride=heads), :].astype(jnp.bfloat16)
        for copy in range(out_ref.shape[0]):
            out_ref[copy, :, head * head_dim : (head + 1) * head_dim] = part


def combine(parts, mean, top, total, lines, copies):
    rows, head_dim = mean.shape
    held = pl.BlockSpec(memory_space=pltpu.VMEM)
    return pl.pallas_call(
        combine_kernel,
        in_specs=[held] * 4,
        out_specs=held,
        out_shape=jax.ShapeDtypeStruct((copies, lines, rows // lines * head_dim), jnp.bfloat16),
        scratch_shapes=[pltpu.VMEM((rows, head_dim), jnp.float32)],
        compiler_params=pltpu.CompilerParams(vmem_limit_bytes=16 * 2**20),
        name="combine_parts",
    )(parts, mean, top, total)


def head_sum_kernel(part_ref, out_ref):
    total = part_ref[0].astype(jnp.float32)
    for head in range(1, part_ref.shape[0]):
        total = total + part_ref[head].astype(jnp.float32)
    steps = out_ref.shape[1]
    for request in range(out_ref.shape[0]):
        rows = total[request * steps : (request + 1) * steps]
        out_ref[request] = rows.astype(jnp.bfloat16)


def head_sum(parts, steps):
    _, rows, columns = parts.shape
    held = pl.BlockSpec(memory_space=pltpu.VMEM)
    return pl.pallas_call(
        head_sum_kernel,
        in_specs=[held],
        out_specs=held,
        out_shape=jax.ShapeDtypeStruct((rows // steps, steps, columns), jnp.bfloat16),
        compiler_params=pltpu.CompilerParams(vmem_limit_bytes=16 * 2**20),
        name="head_sum",
    )(parts)


def shards(
    queries, prefix_keys, prefix_values, suffix_keys, suffix_values, new_keys, new_values,
    suffix_lengths, out_weight,
):
    owned, steps, row_width = queries.shape
    head_dim = prefix_keys.shape[2]
    group_size = row_width // head_dim
    group = owned * steps * group_size
    scale = head_dim**-0.5 * LOG2E
    everyone = owned * lax.axis_size("seq")
    devices = lax.axis_size("seq")
    sharers = devices // 2
    same_core = [list(range(core, devices, 2)) for core in range(2)]
    swap_cores = [(index, index ^ 1) for index in range(devices)]
    own_rows = lax.optimization_barrier(queries.reshape(group, head_dim))
    keys, values = prefix_keys[:, 0, :], prefix_values[:, 0, :]
    gathered = lax.all_to_all(
        jnp.tile(own_rows, (sharers, 1)), "seq", 0, 0, axis_index_groups=same_core, tiled=True
    )
    other_keys = lax.ppermute(keys, "seq", swap_cores)
    other_values = lax.ppermute(values, "seq", swap_cores)
    mean, top, total = suffix_part(
        own_rows.reshape(owned, steps * group_size, head_dim),
        suffix_keys[:, :, 0, :], suffix_values[:, :, 0, :],
        new_keys[:, :, 0, :], new_values[:, :, 0, :], suffix_lengths, group_size, scale,
    )
    parts = prefix_parts(gathered, keys, values, other_keys, other_values, group, scale)
    parts = lax.all_to_all(parts, "seq", 0, 0, axis_index_groups=same_core, tiled=True)
    attended = combine(
        parts, mean.reshape(group, head_dim), top.reshape(group, head_dim),
        total.reshape(group, head_dim), owned * steps, sharers,
    )
    attended = lax.all_to_all(
        attended, "seq", 0, 0, axis_index_groups=same_core, tiled=True
    ).reshape(sharers * owned * steps, row_width)
    other_attended = lax.ppermute(attended, "seq", swap_cores)
    core = lax.axis_index("seq") % 2
    even = jnp.where(core == 0, attended, other_attended)
    odd = jnp.where(core == 0, other_attended, attended)
    attended = jnp.stack(
        [rows.reshape(sharers, owned * steps, row_width) for rows in (even, odd)], axis=1
    ).reshape(everyone * steps, row_width)
    partial = jnp.dot(attended, out_weight, preferred_element_type=jnp.float32)
    columns = out_weight.shape[1]
    heads = lax.axis_size("head")
    partial = partial.astype(jnp.bfloat16).reshape(heads, everyone * steps // heads, columns)
    partial = lax.all_to_all(partial, "head", 0, 0, tiled=True)
    return head_sum(partial, steps)


def solution(mesh):
    placed = (
        P("seq", None, "head"),
        P("seq", "head", None),
        P("seq", "head", None),
        P("seq", None, "head", None),
        P("seq", None, "head", None),
        P("seq", None, "head", None),
        P("seq", None, "head", None),
        P("seq"),
        P("head", "seq"),
    )
    return jax.shard_map(
        shards, mesh=mesh, in_specs=placed, out_specs=P("head", None, "seq"), check_vma=False
    )
```
